256 devices in a mesh: seq: 8 (over z_hi, core), grp: 32 (over y, x, z_lo).
Axes of the slice: x: 4, y: 4, z: 8 (z_hi: 4, z_lo: 2; z = z_hi * 2 + z_lo), core: 2. Of those that a mesh axis runs over, the one named last changes fastest.
Arguments:
- query_first: bfloat16 [16384, 8192], P('seq', 'grp'), may hold values from -6 to 6
- key_first: bfloat16 [16384, 8192], P('seq', 'grp'), may hold values from -6 to 6
- value_first: bfloat16 [16384, 8192], P('seq', 'grp'), may hold values from -6 to 6
- query_second: bfloat16 [16384, 8192], P('seq', 'grp'), may hold values from -6 to 6
- key_second: bfloat16 [16384, 8192], P('seq', 'grp'), may hold values from -6 to 6
- cotangent: bfloat16 [16384, 8192], P('seq', 'grp'), may hold values from -6 to 6
- short_filter: bfloat16 [7, 8192], replicated, may hold values from -2 to 2
- medium_filter: bfloat16 [512, 128], replicated, may hold values from -0.5 to 0.5
Outputs:
- output_second: bfloat16 [16384, 8192], P('seq', 'grp')
- query_first_grad: bfloat16 [16384, 8192], P('seq', 'grp')
- key_first_grad: bfloat16 [16384, 8192], P('seq', 'grp')
- value_first_grad: bfloat16 [16384, 8192], P('seq', 'grp')
- query_second_grad: bfloat16 [16384, 8192], P('seq', 'grp')
- key_second_grad: bfloat16 [16384, 8192], P('seq', 'grp')
- short_filter_grad: float32 [7, 8192], replicated
- medium_filter_grad: float32 [512, 128], replicated
The draws below stay inside these ranges and needn't reach their ends.
All inputs are finite; a program needn't handle non-finite values.
Results may differ from the reference program's by a relative error of at most 0.015.
Values may be sent and summed in bfloat16 or wider, within the bound.
No kernel may reach another device: no remote copies, remote signals or barrier semaphores. Data moves between devices by JAX's collectives and lax.ppermute only.
A program may use at most 64 MiB of HBM per device.

```python
import math
import jax
import jax.numpy as jnp
from jax import lax

D = 8192
GROUP = 16
SE_TAPS = 7
MR_TAPS = 128
TOKENS = 16384
FILTERS = 512


def levels(key, dims, split, least, high):
    factor_of = 1.0
    for axis_at, blocks in split:
        steps = jax.random.uniform(jax.random.fold_in(jax.random.fold_in(key, 6), axis_at), (blocks,), jnp.float32, least / len(split), high / len(split))
        factor_of = factor_of * jnp.repeat(jnp.exp(steps), dims[axis_at] // blocks).reshape((-1,) + (1,) * (len(dims) - 1 - axis_at))
    return factor_of


def scatter_about(rng, extent, spread, most, split=(), kind=jnp.bfloat16):
    level = levels(rng, extent, split, -0.22, 0.18) if split else 1.0
    values = jax.random.normal(rng, extent, jnp.float32) * spread * level
    return jnp.minimum(jnp.maximum(values, -most), most).astype(kind)


def setup_inputs(seed: int = 0) -> dict:
    streams_of = jax.random.split(jax.random.key(seed), 9)
    query_first = scatter_about(streams_of[0], (TOKENS, D), 1.0, 6.0, ((0, 8), (1, 32)))
    key_first = scatter_about(streams_of[1], (TOKENS, D), 1.0, 6.0, ((0, 8), (1, 32)))
    value_first = scatter_about(streams_of[2], (TOKENS, D), 1.0, 6.0, ((0, 8), (1, 32)))
    query_second = scatter_about(streams_of[3], (TOKENS, D), 1.0, 6.0, ((0, 8), (1, 32)))
    key_second = scatter_about(streams_of[4], (TOKENS, D), 1.0, 6.0, ((0, 8), (1, 32)))
    cotangent = scatter_about(streams_of[5], (TOKENS, D), 1.0, 6.0, ((0, 8), (1, 32)))
    short_filter = scatter_about(streams_of[6], (SE_TAPS, D), SE_TAPS ** -0.5, 2.0)
    medium_filter = scatter_about(streams_of[7], (FILTERS, MR_TAPS), MR_TAPS ** -0.5, 0.5)
    return dict(query_first=query_first, key_first=key_first, value_first=value_first, query_second=query_second, key_second=key_second, cotangent=cotangent, short_filter=short_filter, medium_filter=medium_filter)


def widened(array):
    return array.astype(jnp.float32)

def narrowed(array):
    return array.astype(jnp.bfloat16)

def channel_block(index, query_first, key_first, value_first, query_second, key_second, cotangent, short_filter, medium_filter):
    columns = 512
    start = index * columns

    def take(array):
        return lax.dynamic_slice_in_dim(array, start, columns, 1)
    query_one = take(query_first)
    key_one = take(key_first)
    value_one = take(value_first)
    query_two = take(query_second)
    key_two = take(key_second)
    upstream = take(cotangent)
    short_here = take(short_filter)
    group_here = lax.dynamic_slice_in_dim(medium_filter, index * (columns // GROUP), columns // GROUP, 0)
    medium_here = jnp.repeat(group_here, GROUP, axis=0).T
    product_one = narrowed(widened(key_one) * widened(value_one))
    padded_one = jnp.pad(product_one, ((SE_TAPS - 1, 0), (0, 0)))
    inner_one = sum((widened(short_here[shift_by]) * widened(padded_one[SE_TAPS - 1 - shift_by:SE_TAPS - 1 - shift_by + TOKENS]) for shift_by in range(SE_TAPS)))
    gated_one = narrowed(widened(query_one) * inner_one)
    product_two = narrowed(widened(key_two) * widened(gated_one))
    padded_two = jnp.pad(product_two, ((MR_TAPS - 1, 0), (0, 0)))

    def forward_tap(shift_by, total):
        piece = lax.dynamic_slice_in_dim(padded_two, MR_TAPS - 1 - shift_by, TOKENS, 0)
        return total + widened(medium_here[shift_by])[None, :] * widened(piece)
    inner_two = lax.fori_loop(0, MR_TAPS, forward_tap, jnp.zeros((TOKENS, columns), jnp.float32))
    output_two = narrowed(widened(query_two) * inner_two)
    grad_query_two = narrowed(widened(upstream) * inner_two)
    grad_inner_two = narrowed(widened(upstream) * widened(query_two))
    trailing_two = jnp.pad(grad_inner_two, ((0, MR_TAPS - 1), (0, 0)))

    def backward_tap(shift_by, total):
        piece = lax.dynamic_slice_in_dim(trailing_two, shift_by, TOKENS, 0)
        return total + widened(medium_here[shift_by])[None, :] * widened(piece)
    grad_product_two = lax.fori_loop(0, MR_TAPS, backward_tap, jnp.zeros((TOKENS, columns), jnp.float32))

    def filter_tap(shift_by, table):
        piece = lax.dynamic_slice_in_dim(padded_two, MR_TAPS - 1 - shift_by, TOKENS, 0)
        return table.at[shift_by].set(lax.optimization_barrier(jnp.sum(widened(grad_inner_two) * widened(piece), axis=0)))
    medium_table = lax.fori_loop(0, MR_TAPS, filter_tap, jnp.zeros((MR_TAPS, columns), jnp.float32))
    medium_grad = medium_table.T.reshape(columns // GROUP, GROUP, MR_TAPS).sum(axis=1)
    grad_key_two = narrowed(grad_product_two * widened(gated_one))
    grad_gated_one = grad_product_two * widened(key_two)
    grad_query_one = narrowed(grad_gated_one * inner_one)
    grad_inner_one = narrowed(grad_gated_one * widened(query_one))
    trailing_one = jnp.pad(grad_inner_one, ((0, SE_TAPS - 1), (0, 0)))
    grad_product_one = sum((widened(short_here[shift_by]) * widened(trailing_one[shift_by:shift_by + TOKENS]) for shift_by in range(SE_TAPS)))
    grad_key_one = narrowed(grad_product_one * widened(value_one))
    grad_value_one = narrowed(grad_product_one * widened(key_one))
    short_grad = jnp.stack([lax.optimization_barrier(jnp.sum(widened(grad_inner_one) * widened(padded_one[SE_TAPS - 1 - shift_by:SE_TAPS - 1 - shift_by + TOKENS]), axis=0)) for shift_by in range(SE_TAPS)])
    return (output_two, grad_query_one, grad_key_one, grad_value_one, grad_query_two, grad_key_two, short_grad, medium_grad)

def reference(query_first, key_first, value_first, query_second, key_second, cotangent, short_filter, medium_filter):
    block_count = D // 512

    def one_block(index):
        return channel_block(index, query_first, key_first, value_first, query_second, key_second, cotangent, short_filter, medium_filter)
    results = lax.map(one_block, jnp.arange(block_count).astype(jnp.int32))

    def unblock(stacked):
        return stacked.transpose(1, 0, 2).reshape(TOKENS, D)
    short_grad = results[6].transpose(1, 0, 2).reshape(SE_TAPS, D) * (1.0 / math.sqrt(TOKENS))
    medium_grad = results[7].reshape(FILTERS, MR_TAPS) * (1.0 / math.sqrt(TOKENS * GROUP))
    return (unblock(results[0]), unblock(results[1]), unblock(results[2]), unblock(results[3]), unblock(results[4]), unblock(results[5]), short_grad, medium_grad)
```

```python
import functools
import math

import jax
import jax.numpy as jnp
from jax import lax
from jax.experimental import pallas as pl
from jax.experimental.pallas import tpu as pltpu
from jax.sharding import PartitionSpec as P

GROUP = 16
SE_TAPS = 7
MR_TAPS = 128
BLOCK = 128
LANES = 128
RIM = 8
HALO = 16
VMEM_LIMIT = 63 * 1024 * 1024


def widened(array):
    return array.astype(jnp.float32)


def narrowed(array):
    return array.astype(jnp.bfloat16)


def passed_along(value, axis, steps):
    count = lax.axis_size(axis)
    first, last = (max(0, -steps), min(count, count - steps))
    return lax.ppermute(value, axis, [(source, source + steps) for source in range(first, last)])


def rows_of(index, count):
    return pl.ds(pl.multiple_of(index * count, count), count)


def short_causal(prior, here, taps):
    ext = jnp.concatenate([prior, here], axis=0)
    total = taps[0:1] * here
    for shift_by in range(1, SE_TAPS):
        total += taps[shift_by : shift_by + 1] * pltpu.roll(ext, shift_by, 0)[RIM:]
    return total


def upper_lower(coefs):
    line = jnp.concatenate([coefs, jnp.zeros_like(coefs)], axis=1)
    table = jnp.broadcast_to(line, (BLOCK, 2 * BLOCK))
    return narrowed(pltpu.roll(table, 0, 1, stride=1, stride_axis=0))


def dotted(left, right, dims):
    return lax.dot_general(left, right, (dims, ((), ())), preferred_element_type=jnp.float32)


def turned(tile):
    return tile.T.reshape(LANES // GROUP, GROUP, BLOCK)


def rims_kernel(
    key_tail, value_tail, query_tail, key_two_tail,
    cotangent_head, query_two_head, query_head, key_two_head,
    short_ref, medium_ref, tail_ref, head_ref,
):
    taps = widened(short_ref[...])
    start = 2 * BLOCK - BLOCK - HALO
    product_one = widened(key_tail[start:]) * widened(value_tail[start:])
    inner_one = short_causal(product_one[RIM:HALO], product_one[HALO:], taps)
    product_two = widened(key_two_tail[BLOCK:]) * (widened(query_tail[BLOCK:]) * inner_one)
    tail_ref[:HALO] = narrowed(product_one[BLOCK:])
    tail_ref[HALO:] = narrowed(product_two)
    grad_inner = narrowed(
        widened(cotangent_head[: BLOCK + HALO]) * widened(query_two_head[: BLOCK + HALO])
    )
    head_ref[:BLOCK] = grad_inner[:BLOCK]
    wide = widened(grad_inner)
    chan_count = wide.shape[1]
    group_count = chan_count // GROUP
    owner = lax.broadcasted_iota(jnp.int32, (group_count, chan_count), 1) // GROUP
    spread = narrowed(widened(owner == lax.broadcasted_iota(jnp.int32, owner.shape, 0)))
    coefs = dotted(widened(medium_ref[...]).T, widened(spread), ((1,), (0,)))
    row = lax.broadcasted_iota(jnp.int32, (HALO, chan_count), 0)
    grad_product = jnp.zeros((HALO, chan_count), jnp.float32)
    for shift_by in range(SE_TAPS - 1):
        moved = wide[:BLOCK]
        if shift_by:
            moved = pltpu.roll(wide, BLOCK + HALO - shift_by, 0)[:BLOCK]
        line = jnp.sum(coefs * moved, axis=0, keepdims=True)
        grad_product = jnp.where(row == shift_by, line, grad_product)
    head_ref[BLOCK:] = narrowed(
        grad_product * widened(key_two_head[...]) * widened(query_head[...])
    )


def gradient_kernel(
    query_ref, key_ref, value_ref, query_two_ref, key_two_ref, cotangent_ref,
    short_ref, medium_ref, tail_ref, head_ref,
    query_grad_ref, key_two_grad_ref, product_ref, grad_inner_ref, parts_ref,
    inner_ref, first_ref, later_ref, turned_ref, back_ref,
):
    row_count = query_ref.shape[0]
    block_count = row_count // BLOCK
    group_count = LANES // GROUP
    taps = widened(short_ref[...])
    sequence_total = row_count * lax.axis_size("seq")

    product_ref[:, :GROUP, :] = turned(tail_ref[HALO:])
    turned_ref[:, block_count * GROUP :, :] = turned(head_ref[:BLOCK])
    grad_inner_ref[row_count:] = head_ref[BLOCK:]

    def forward(index, _):
        rows = rows_of(index, BLOCK)
        product_one = widened(key_ref[rows]) * widened(value_ref[rows])
        first_ref[pl.ds(pl.multiple_of(index * BLOCK + RIM, RIM), BLOCK)] = product_one
        inner_one = taps[0:1] * product_one
        for shift_by in range(1, SE_TAPS):
            inner_one += (
                taps[shift_by : shift_by + 1]
                * first_ref[pl.ds(index * BLOCK + RIM - shift_by, BLOCK)]
            )
        inner_ref[rows] = inner_one
        product_two = narrowed(
            widened(key_two_ref[rows]) * (widened(query_ref[rows]) * inner_one)
        )
        product_ref[:, rows_of(index + 1, GROUP), :] = turned(product_two)
        grad_inner_two = narrowed(widened(cotangent_ref[rows]) * widened(query_two_ref[rows]))
        turned_ref[:, rows_of(index, GROUP), :] = turned(grad_inner_two)
        return 0

    first_ref[:RIM] = widened(tail_ref[RIM:HALO])
    lax.fori_loop(0, block_count, forward, 0)

    span = block_count * GROUP
    flip_row = lax.broadcasted_iota(jnp.int32, (BLOCK, BLOCK), 0)
    flip_lane = lax.broadcasted_iota(jnp.int32, (BLOCK, BLOCK), 1)
    flip = narrowed(widened(flip_row + flip_lane == BLOCK - 1))
    medium_scale = 1.0 / math.sqrt(sequence_total * GROUP)
    for group in range(group_count):
        bands = upper_lower(widened(medium_ref[group : group + 1]))
        window = jnp.concatenate(
            [turned_ref[group, :span], turned_ref[group, GROUP : GROUP + span]], axis=1
        )
        back_ref[group] = narrowed(dotted(window, bands, ((1,), (1,))))
        flipped = narrowed(dotted(flip, product_ref[group, GROUP:], ((1,), (1,))))
        pairs = dotted(flipped, window, ((1,), (0,)))
        pairs = pltpu.roll(pairs, BLOCK + 1, 1, stride=1, stride_axis=0)
        line = jnp.sum(pairs[:, :BLOCK], axis=0, keepdims=True) * medium_scale
        parts_ref[:, RIM + group : RIM + group + 1, :] = jnp.broadcast_to(
            line[None], (parts_ref.shape[0], 1, LANES)
        )

    def backward(step, sums):
        index = block_count - 1 - step
        rows = rows_of(index, BLOCK)
        turned_back = back_ref[:, rows_of(index, GROUP), :].reshape(LANES, BLOCK)
        grad_product = widened(turned_back.T)
        inner_one = inner_ref[rows]
        query = widened(query_ref[rows])
        key_two_grad_ref[rows] = narrowed(grad_product * (query * inner_one))
        grad_gated = grad_product * widened(key_two_ref[rows])
        query_grad_ref[rows] = narrowed(grad_gated * inner_one)
        grad_inner = grad_gated * query
        grad_inner_ref[rows] = narrowed(grad_inner)
        later_ref[rows] = grad_inner
        product_one = first_ref[pl.ds(pl.multiple_of(index * BLOCK + RIM, RIM), BLOCK)]
        moved = [grad_inner] + [
            later_ref[pl.ds(index * BLOCK + shift_by, BLOCK)] for shift_by in range(1, SE_TAPS)
        ]
        return [
            total + jnp.sum((product_one * other).reshape(BLOCK // RIM, RIM, LANES), axis=0)
            for total, other in zip(sums, moved)
        ]

    later_ref[row_count:] = widened(head_ref[BLOCK:])[:RIM]
    sums = lax.fori_loop(
        0, block_count, backward, [jnp.zeros((RIM, LANES), jnp.float32)] * SE_TAPS
    )
    short_scale = 1.0 / math.sqrt(sequence_total)
    lines = [jnp.sum(total, axis=0, keepdims=True) * short_scale for total in sums]
    lines = jnp.concatenate(lines + [jnp.zeros_like(lines[0])], axis=0)
    parts_ref[:, :RIM, :] = jnp.broadcast_to(lines[None], (parts_ref.shape[0], RIM, LANES))


def medium_kernel(
    product_ref, query_two_ref, cotangent_ref, medium_ref, output_ref, query_grad_ref, inner_ref
):
    block_count = query_two_ref.shape[0] // BLOCK
    span = block_count * GROUP
    for group in range(LANES // GROUP):
        bands = upper_lower(widened(medium_ref[group : group + 1]))
        inner_ref[group] = narrowed(
            dotted(product_ref[group, :span], bands[:, BLOCK:], ((1,), (0,)))
            + dotted(product_ref[group, GROUP:], bands[:, :BLOCK], ((1,), (0,)))
        )

    def one_block(index, _):
        rows = rows_of(index, BLOCK)
        inner_two = widened(inner_ref[:, rows_of(index, GROUP), :].reshape(LANES, BLOCK).T)
        output_ref[rows] = narrowed(widened(query_two_ref[rows]) * inner_two)
        query_grad_ref[rows] = narrowed(widened(cotangent_ref[rows]) * inner_two)
        return 0

    lax.fori_loop(0, block_count, one_block, 0)


def short_kernel(
    grad_inner_ref, key_ref, value_ref, short_ref, key_grad_ref, value_grad_ref, later_ref
):
    taps = widened(short_ref[...])
    block_count = key_ref.shape[0] // BLOCK

    row_count = key_ref.shape[0]
    later_ref[row_count:] = widened(grad_inner_ref[row_count:])[:RIM]

    def one_block(step, _):
        index = block_count - 1 - step
        rows = rows_of(index, BLOCK)
        here = widened(grad_inner_ref[rows])
        later_ref[rows] = here
        total = taps[0:1] * here
        for shift_by in range(1, SE_TAPS):
            total += (
                taps[shift_by : shift_by + 1] * later_ref[pl.ds(index * BLOCK + shift_by, BLOCK)]
            )
        key_grad_ref[rows] = narrowed(total * widened(value_ref[rows]))
        value_grad_ref[rows] = narrowed(total * widened(key_ref[rows]))
        return 0

    lax.fori_loop(0, block_count, one_block, 0)


def unpack_kernel(table_ref, short_ref, medium_ref):
    chan_count = table_ref.shape[2]
    groups = LANES // GROUP
    for place in range(table_ref.shape[0]):
        piece = widened(table_ref[place])
        short_ref[:, place * chan_count : (place + 1) * chan_count] = piece[:SE_TAPS]
        for half in range(chan_count // LANES):
            first = (place * (chan_count // LANES) + half) * groups
            medium_ref[first : first + groups] = piece[RIM:, half * LANES : (half + 1) * LANES]


def gather_groups(count):
    run = min(8, count)
    near = [list(range(first, first + run)) for first in range(0, count, run)]
    far = [list(range(first, count, run)) for first in range(run)]
    return near, far


def params():
    return pltpu.CompilerParams(vmem_limit_bytes=VMEM_LIMIT)


def cost(flops, size):
    return pl.CostEstimate(flops=flops, bytes_accessed=size, transcendentals=0)


def per_device(
    query_first,
    key_first,
    value_first,
    query_second,
    key_second,
    cotangent,
    short_filter,
    medium_filter,
):
    row_count, chan_count = query_first.shape
    group_count = chan_count // GROUP
    block_count = row_count // BLOCK
    halves = chan_count // LANES
    half_groups = LANES // GROUP
    group_index = lax.axis_index("grp")
    short_here = lax.dynamic_slice_in_dim(short_filter, group_index * chan_count, chan_count, 1)
    medium_here = lax.dynamic_slice_in_dim(medium_filter, group_index * group_count, group_count, 0)
    sds = jax.ShapeDtypeStruct
    wide = sds((row_count, chan_count), jnp.bfloat16)
    size = row_count * chan_count * 2

    last = row_count // (2 * BLOCK) - 1
    tail_spec = pl.BlockSpec((2 * BLOCK, chan_count), lambda i: (last, 0))
    head_spec = pl.BlockSpec((2 * BLOCK, chan_count), lambda i: (0, 0))
    rim_spec = pl.BlockSpec((HALO, chan_count), lambda i: (0, 0))
    halo_spec = pl.BlockSpec((HALO + BLOCK, chan_count), lambda i: (0, 0))
    halo = sds((HALO + BLOCK, chan_count), jnp.bfloat16)
    tail, head = pl.pallas_call(
        rims_kernel,
        grid=(1,),
        out_shape=(halo, halo),
        in_specs=[tail_spec] * 4
        + [head_spec] * 2
        + [rim_spec] * 2
        + [
            pl.BlockSpec((SE_TAPS, chan_count), lambda i: (0, 0)),
            pl.BlockSpec((group_count, MR_TAPS), lambda i: (0, 0)),
        ],
        out_specs=(halo_spec, halo_spec),
        compiler_params=params(),
        cost_estimate=cost(2 * 6 * 2 * BLOCK * chan_count * 16, size),
        name="rims",
    )(
        key_first, value_first, query_first, key_second,
        cotangent, query_second, query_first, key_second,
        short_here, medium_here,
    )
    tail = passed_along(tail, "seq", 1)
    head = passed_along(head, "seq", -1)

    full_spec = pl.BlockSpec((row_count, LANES), lambda i: (0, i))
    short_spec = pl.BlockSpec((SE_TAPS, LANES), lambda i: (0, i))
    medium_spec = pl.BlockSpec((half_groups, MR_TAPS), lambda i: (i, 0))
    half_halo = pl.BlockSpec((HALO + BLOCK, LANES), lambda i: (0, i))
    lines = (block_count + 1) * GROUP
    product_spec = pl.BlockSpec((half_groups, lines, BLOCK), lambda i: (i, 0, 0))
    inner_spec = pl.BlockSpec((row_count + HALO, LANES), lambda i: (0, i))
    seq_count = lax.axis_size("seq")
    parts_spec = pl.BlockSpec((seq_count, 2 * RIM, LANES), lambda i: (0, 0, i))
    query_first_grad, key_second_grad, product_two, grad_inner_one, parts = pl.pallas_call(
        gradient_kernel,
        grid=(halves,),
        out_shape=(
            wide,
            wide,
            sds((group_count, lines, BLOCK), jnp.bfloat16),
            sds((row_count + HALO, chan_count), jnp.bfloat16),
            sds((seq_count, 2 * RIM, chan_count), jnp.float32),
        ),
        in_specs=[full_spec] * 6 + [short_spec, medium_spec, half_halo, half_halo],
        out_specs=(full_spec, full_spec, product_spec, inner_spec, parts_spec),
        scratch_shapes=[
            pltpu.VMEM((row_count, LANES), jnp.float32),
            pltpu.VMEM((row_count + RIM, LANES), jnp.float32),
            pltpu.VMEM((row_count + RIM, LANES), jnp.float32),
            pltpu.VMEM((half_groups, lines, BLOCK), jnp.bfloat16),
            pltpu.VMEM((half_groups, lines - GROUP, BLOCK), jnp.bfloat16),
        ],
        compiler_params=params(),
        cost_estimate=cost(100 * row_count * chan_count, 10 * size),
        name="gradients",
    )(
        query_first, key_first, value_first, query_second, key_second, cotangent,
        short_here, medium_here, tail, head,
    )

    partials = lax.all_to_all(parts, "seq", 0, 0)

    output_second, query_second_grad = pl.pallas_call(
        medium_kernel,
        grid=(halves,),
        out_shape=(wide, wide),
        in_specs=[product_spec, full_spec, full_spec, medium_spec],
        out_specs=(full_spec, full_spec),
        scratch_shapes=[pltpu.VMEM((half_groups, lines - GROUP, BLOCK), jnp.bfloat16)],
        compiler_params=params(),
        cost_estimate=cost(40 * row_count * chan_count, 5 * size),
        name="medium_outputs",
    )(product_two, query_second, cotangent, medium_here)
    partials, output_second, query_second_grad = lax.optimization_barrier(
        (partials, output_second, query_second_grad)
    )
    sums = narrowed(jnp.sum(partials, axis=0))
    near, far = gather_groups(lax.axis_size("grp"))
    copies = jnp.broadcast_to(sums[None], (len(near[0]), *sums.shape))
    table = lax.all_to_all(copies, "grp", 0, 0, axis_index_groups=near)
    copies = jnp.broadcast_to(table[None], (len(far[0]), *table.shape))
    table = lax.all_to_all(copies, "grp", 0, 0, axis_index_groups=far)
    table = table.reshape(-1, *sums.shape)
    key_first_grad, value_first_grad = pl.pallas_call(
        short_kernel,
        grid=(halves,),
        out_shape=(wide, wide),
        in_specs=[inner_spec, full_spec, full_spec, short_spec],
        out_specs=(full_spec, full_spec),
        scratch_shapes=[pltpu.VMEM((row_count + RIM, LANES), jnp.float32)],
        compiler_params=params(),
        cost_estimate=cost(40 * row_count * chan_count, 5 * size),
        name="short_outputs",
    )(grad_inner_one, key_first, value_first, short_here)

    short_grad, medium_grad = pl.pallas_call(
        unpack_kernel,
        out_shape=(
            sds(short_filter.shape, jnp.float32),
            sds(medium_filter.shape, jnp.float32),
        ),
        compiler_params=params(),
        name="unpack",
    )(table)
    return (
        output_second,
        query_first_grad,
        key_first_grad,
        value_first_grad,
        query_second_grad,
        key_second_grad,
        short_grad,
        medium_grad,
    )


def solution(mesh):
    return jax.shard_map(
        per_device,
        mesh=mesh,
        in_specs=(
            *(P("seq", "grp"),) * 6,
            P(None, None),
            P(None, None),
        ),
        out_specs=(*(P("seq", "grp"),) * 6, P(None, None), P(None, None)),
        check_vma=False,
    )
```

```python
import functools
import math

import jax
import jax.numpy as jnp
from jax import lax
from jax.experimental import pallas as pl
from jax.experimental.pallas import tpu as pltpu
from jax.sharding import PartitionSpec as P

GROUP = 16
SE_TAPS = 7
MR_TAPS = 128
BLOCK = 128
LANES = 128
RIM = 8
CHUNK = 256
HALO = 16
VMEM_LIMIT = 63 * 1024 * 1024


def widened(array):
    return array.astype(jnp.float32)


def narrowed(array):
    return array.astype(jnp.bfloat16)


def passed_along(value, axis, steps):
    count = lax.axis_size(axis)
    first, last = (max(0, -steps), min(count, count - steps))
    return lax.ppermute(value, axis, [(source, source + steps) for source in range(first, last)])


def rows_of(index, count):
    return pl.ds(pl.multiple_of(index * count, count), count)


def short_causal(prior, here, taps):
    ext = jnp.concatenate([prior, here], axis=0)
    total = taps[0:1] * here
    for shift_by in range(1, SE_TAPS):
        total += taps[shift_by : shift_by + 1] * pltpu.roll(ext, shift_by, 0)[RIM:]
    return total


def upper_lower(coefs):
    line = jnp.concatenate([coefs, jnp.zeros_like(coefs)], axis=1)
    table = jnp.broadcast_to(line, (BLOCK, 2 * BLOCK))
    return narrowed(pltpu.roll(table, 0, 1, stride=1, stride_axis=0))


def dotted(left, right, dims):
    return lax.dot_general(left, right, (dims, ((), ())), preferred_element_type=jnp.float32)


def identity(count):
    row = lax.broadcasted_iota(jnp.int32, (count, count), 0)
    lane = lax.broadcasted_iota(jnp.int32, (count, count), 1)
    return narrowed(widened(row == lane))


def turned(tile, unit):
    flat = narrowed(dotted(unit, tile, ((1,), (1,))))
    return flat.reshape(tile.shape[1] // GROUP, GROUP, tile.shape[0])


def rims_kernel(
    place_ref,
    key_tail, value_tail, query_tail, key_two_tail,
    cotangent_head, query_two_head, query_head, key_two_head,
    short_ref, medium_ref, tail_ref, head_ref,
):
    taps = widened(short_ref[...])
    start = 2 * BLOCK - BLOCK - HALO
    product_one = widened(key_tail[start:]) * widened(value_tail[start:])
    inner_one = short_causal(product_one[RIM:HALO], product_one[HALO:], taps)
    product_two = widened(key_two_tail[BLOCK:]) * (widened(query_tail[BLOCK:]) * inner_one)
    tail_ref[:HALO] = narrowed(product_one[BLOCK:])
    tail_ref[HALO:] = narrowed(product_two)
    grad_inner = narrowed(
        widened(cotangent_head[: BLOCK + HALO]) * widened(query_two_head[: BLOCK + HALO])
    )
    head_ref[:BLOCK] = grad_inner[:BLOCK]
    wide = widened(grad_inner)
    chan_count = wide.shape[1]
    group_count = chan_count // GROUP
    owner = lax.broadcasted_iota(jnp.int32, (group_count, chan_count), 1) // GROUP
    spread = narrowed(widened(owner == lax.broadcasted_iota(jnp.int32, owner.shape, 0)))
    coefs = dotted(widened(medium_ref[...]).T, widened(spread), ((1,), (0,)))
    row = lax.broadcasted_iota(jnp.int32, (HALO, chan_count), 0)
    grad_product = jnp.zeros((HALO, chan_count), jnp.float32)
    for shift_by in range(SE_TAPS - 1):
        moved = wide[:BLOCK]
        if shift_by:
            moved = pltpu.roll(wide, BLOCK + HALO - shift_by, 0)[:BLOCK]
        line = jnp.sum(coefs * moved, axis=0, keepdims=True)
        grad_product = jnp.where(row == shift_by, line, grad_product)
    head_ref[BLOCK:] = narrowed(
        grad_product * widened(key_two_head[...]) * widened(query_head[...])
    )


def main_kernel(
    place_ref,
    query_any, key_any, value_any, query_two_any, key_two_any, cotangent_any,
    short_ref, medium_ref, tail_ref, head_ref,
    output_any, query_grad_any, key_grad_any, value_grad_any, query_two_grad_any, key_two_grad_any,
    parts_ref,
    query_ref, key_ref, value_ref, query_two_ref, key_two_ref, cotangent_ref,
    output_ref, query_grad_ref, key_grad_ref, value_grad_ref, query_two_grad_ref, key_two_grad_ref,
    inner_ref, gated_ref, first_ref, later_ref, pair_ref, product_ref, turned_ref, back_ref, ahead_ref,
    sums_ref, in_sems, out_sems,
):
    row_count, chan_count = query_ref.shape
    group_count = chan_count // GROUP
    chunk_count = row_count // CHUNK
    span = row_count // BLOCK * GROUP
    halves = chan_count // LANES
    steps = CHUNK // BLOCK
    taps = widened(short_ref[...])
    sequence_total = row_count * lax.axis_size("seq")
    sources = (key_any, value_any, query_any, key_two_any, cotangent_any, query_two_any)
    buffers = (key_ref, value_ref, query_ref, key_two_ref, cotangent_ref, query_two_ref)
    results = (
        output_ref, query_grad_ref, key_grad_ref, value_grad_ref, query_two_grad_ref, key_two_grad_ref
    )
    targets = (
        output_any, query_grad_any, key_grad_any, value_grad_any, query_two_grad_any, key_two_grad_any
    )

    def copies_in(chunk):
        rows = rows_of(chunk, CHUNK)
        return [
            pltpu.make_async_copy(source.at[rows], buffer.at[rows], in_sems.at[place, chunk])
            for place, (source, buffer) in enumerate(zip(sources, buffers))
        ]

    def copies_out(chunk):
        rows = rows_of(chunk, CHUNK)
        return [
            pltpu.make_async_copy(result.at[rows], target.at[rows], out_sems.at[place, chunk])
            for place, (result, target) in enumerate(zip(results, targets))
        ]

    def start_in(chunk, _):
        for copy in copies_in(chunk):
            copy.start()
        return 0

    lax.fori_loop(0, chunk_count, start_in, 0)

    unit = identity(chan_count)
    small_unit = unit[:BLOCK, :BLOCK]
    product_ref[:, :GROUP, :] = turned(tail_ref[HALO:], unit)
    turned_ref[:, span:, :] = turned(head_ref[:BLOCK], unit)
    for half in range(halves):
        lanes = slice(half * LANES, (half + 1) * LANES)
        first_ref[half, :RIM] = widened(tail_ref[:HALO, lanes])[RIM:]
        later_ref[half, row_count:] = widened(head_ref[BLOCK:, lanes])[:RIM]

    def forward(chunk, _):
        for copy in copies_in(chunk):
            copy.wait()
        for step in range(steps):
            index = chunk * steps + step
            rows = rows_of(index, BLOCK)
            local = slice(step * BLOCK, (step + 1) * BLOCK)
            for half in range(halves):
                lanes = slice(half * LANES, (half + 1) * LANES)
                product_one = widened(key_ref[rows, lanes] * value_ref[rows, lanes])
                first_ref[half, pl.ds(pl.multiple_of(index * BLOCK + RIM, RIM), BLOCK)] = product_one
                inner_one = taps[0:1, lanes] * product_one
                for shift_by in range(1, SE_TAPS):
                    inner_one += (
                        taps[shift_by : shift_by + 1, lanes]
                        * first_ref[half, pl.ds(index * BLOCK + RIM - shift_by, BLOCK)]
                    )
                inner_one = narrowed(inner_one)
                gated = query_ref[rows, lanes] * inner_one
                inner_ref[rows, lanes] = inner_one
                gated_ref[rows, lanes] = gated
                pair_ref[0, local, lanes] = key_two_ref[rows, lanes] * gated
                pair_ref[1, local, lanes] = cotangent_ref[rows, lanes] * query_two_ref[rows, lanes]
        product_two = turned(pair_ref[0], unit)
        grad_inner_two = turned(pair_ref[1], unit)
        for step in range(steps):
            index = chunk * steps + step
            local = slice(step * BLOCK, (step + 1) * BLOCK)
            product_ref[:, rows_of(index + 1, GROUP), :] = product_two[:, :, local]
            turned_ref[:, rows_of(index, GROUP), :] = grad_inner_two[:, :, local]
        return 0

    lax.fori_loop(0, chunk_count, forward, 0)

    flip_row = lax.broadcasted_iota(jnp.int32, (BLOCK, BLOCK), 0)
    flip_lane = lax.broadcasted_iota(jnp.int32, (BLOCK, BLOCK), 1)
    flip = narrowed(widened(flip_row + flip_lane == BLOCK - 1))
    medium_scale = 1.0 / math.sqrt(sequence_total * GROUP)
    for group in range(group_count):
        bands = upper_lower(widened(medium_ref[group : group + 1]))
        window = jnp.concatenate(
            [turned_ref[group, :span], turned_ref[group, GROUP : GROUP + span]], axis=1
        )
        back_ref[group] = narrowed(dotted(window, bands, ((1,), (1,))))
        earlier = jnp.concatenate([product_ref[group, :span], product_ref[group, GROUP:]], axis=1)
        causal = jnp.concatenate([bands[:, BLOCK:], bands[:, :BLOCK]], axis=0)
        ahead_ref[group] = narrowed(dotted(earlier, causal, ((1,), (0,))))
        flipped = narrowed(dotted(flip, product_ref[group, GROUP:], ((1,), (1,))))
        pairs = dotted(flipped, window, ((1,), (0,)))
        pairs = pltpu.roll(pairs, BLOCK + 1, 1, stride=1, stride_axis=0)
        line = jnp.sum(pairs[:, :BLOCK], axis=0, keepdims=True) * medium_scale
        half, row = group * GROUP // LANES, RIM + group % (LANES // GROUP)
        parts_ref[:, row : row + 1, half * LANES : (half + 1) * LANES] = jnp.broadcast_to(
            line[None], (parts_ref.shape[0], 1, LANES)
        )

    sums_ref[...] = jnp.zeros_like(sums_ref)

    def backward(turn, _):
        chunk = chunk_count - 1 - turn
        for step in reversed(range(steps)):
            index = chunk * steps + step
            rows = rows_of(index, BLOCK)
            lines = rows_of(index, GROUP)
            back = back_ref[:, lines, :].reshape(chan_count, BLOCK)
            ahead = ahead_ref[:, lines, :].reshape(chan_count, BLOCK)
            back = narrowed(dotted(small_unit, back, ((1,), (1,))))
            ahead = narrowed(dotted(small_unit, ahead, ((1,), (1,))))
            output_ref[rows] = query_two_ref[rows] * ahead
            query_two_grad_ref[rows] = cotangent_ref[rows] * ahead
            key_two_grad_ref[rows] = back * gated_ref[rows]
            grad_gated = back * key_two_ref[rows]
            query_grad_ref[rows] = grad_gated * inner_ref[rows]
            grad_inner = widened(grad_gated * query_ref[rows])
            for half in range(halves):
                lanes = slice(half * LANES, (half + 1) * LANES)
                here = grad_inner[:, lanes]
                later_ref[half, rows] = here
                product_one = first_ref[half, pl.ds(pl.multiple_of(index * BLOCK + RIM, RIM), BLOCK)]
                total = jnp.zeros_like(here)
                for shift_by in range(SE_TAPS):
                    moved = here
                    if shift_by:
                        moved = later_ref[half, pl.ds(index * BLOCK + shift_by, BLOCK)]
                    total += taps[shift_by : shift_by + 1, lanes] * moved
                    sums_ref[half, shift_by] += jnp.sum(
                        (product_one * moved).reshape(BLOCK // RIM, RIM, LANES), axis=0
                    )
                total = narrowed(total)
                key_grad_ref[rows, lanes] = total * value_ref[rows, lanes]
                value_grad_ref[rows, lanes] = total * key_ref[rows, lanes]
        for copy in copies_out(chunk):
            copy.start()
        return 0

    lax.fori_loop(0, chunk_count, backward, 0)

    short_scale = 1.0 / math.sqrt(sequence_total)
    for half in range(halves):
        lines = [
            jnp.sum(sums_ref[half, shift_by], axis=0, keepdims=True) * short_scale
            for shift_by in range(SE_TAPS)
        ]
        lines = jnp.concatenate(lines + [jnp.zeros_like(lines[0])], axis=0)
        parts_ref[:, :RIM, half * LANES : (half + 1) * LANES] = jnp.broadcast_to(
            lines[None], (parts_ref.shape[0], RIM, LANES)
        )

    def wait_out(chunk, _):
        for copy in copies_out(chunk):
            copy.wait()
        return 0

    lax.fori_loop(0, chunk_count, wait_out, 0)


def unpack_kernel(table_ref, short_ref, medium_ref):
    chan_count = table_ref.shape[2]
    groups = LANES // GROUP
    for place in range(table_ref.shape[0]):
        piece = widened(table_ref[place])
        short_ref[:, place * chan_count : (place + 1) * chan_count] = piece[:SE_TAPS]
        for half in range(chan_count // LANES):
            first = (place * (chan_count // LANES) + half) * groups
            medium_ref[first : first + groups] = piece[RIM:, half * LANES : (half + 1) * LANES]


def params():
    return pltpu.CompilerParams(vmem_limit_bytes=VMEM_LIMIT)


def cost(flops, size):
    return pl.CostEstimate(flops=flops, bytes_accessed=size, transcendentals=0)


def per_device(
    query_first,
    key_first,
    value_first,
    query_second,
    key_second,
    cotangent,
    short_filter,
    medium_filter,
):
    row_count, chan_count = query_first.shape
    group_count = chan_count // GROUP
    place = lax.axis_index("grp").astype(jnp.int32).reshape(1)
    sds = jax.ShapeDtypeStruct
    wide = sds((row_count, chan_count), jnp.bfloat16)
    size = row_count * chan_count * 2

    last = row_count // (2 * BLOCK) - 1
    tail_spec = pl.BlockSpec((2 * BLOCK, chan_count), lambda i, at: (last, 0))
    head_spec = pl.BlockSpec((2 * BLOCK, chan_count), lambda i, at: (0, 0))
    rim_spec = pl.BlockSpec((HALO, chan_count), lambda i, at: (0, 0))
    halo_spec = pl.BlockSpec((HALO + BLOCK, chan_count), lambda i, at: (0, 0))
    short_spec = pl.BlockSpec((SE_TAPS, chan_count), lambda i, at: (0, at[0]))
    medium_spec = pl.BlockSpec((group_count, MR_TAPS), lambda i, at: (at[0], 0))
    halo = sds((HALO + BLOCK, chan_count), jnp.bfloat16)
    tail, head = pl.pallas_call(
        rims_kernel,
        grid_spec=pltpu.PrefetchScalarGridSpec(
            num_scalar_prefetch=1,
            grid=(1,),
            in_specs=[tail_spec] * 4 + [head_spec] * 2 + [rim_spec] * 2 + [short_spec, medium_spec],
            out_specs=(halo_spec, halo_spec),
        ),
        out_shape=(halo, halo),
        compiler_params=params(),
        cost_estimate=cost(2 * 6 * 2 * BLOCK * chan_count * 16, size),
        name="rims",
    )(
        place,
        key_first, value_first, query_first, key_second,
        cotangent, query_second, query_first, key_second,
        short_filter, medium_filter,
    )
    tail = passed_along(tail, "seq", 1)
    head = passed_along(head, "seq", -1)

    any_spec = pl.BlockSpec(memory_space=pl.ANY)
    seq_count = lax.axis_size("seq")
    lines = (row_count // BLOCK + 1) * GROUP
    halves = chan_count // LANES
    stream = pltpu.VMEM((row_count, chan_count), jnp.bfloat16)
    turned_stream = pltpu.VMEM((group_count, lines, BLOCK), jnp.bfloat16)
    results = pl.pallas_call(
        main_kernel,
        grid_spec=pltpu.PrefetchScalarGridSpec(
            num_scalar_prefetch=1,
            grid=(1,),
            in_specs=[any_spec] * 6 + [short_spec, medium_spec, halo_spec, halo_spec],
            out_specs=(any_spec,) * 6
            + (pl.BlockSpec((seq_count, 2 * RIM, chan_count), lambda i, at: (0, 0, 0)),),
            scratch_shapes=[stream] * 14
            + [pltpu.VMEM((halves, row_count + RIM, LANES), jnp.float32)] * 2
            + [pltpu.VMEM((2, CHUNK, chan_count), jnp.bfloat16)]
            + [turned_stream] * 2
            + [pltpu.VMEM((group_count, lines - GROUP, BLOCK), jnp.bfloat16)] * 2
            + [pltpu.VMEM((halves, SE_TAPS, RIM, LANES), jnp.float32)]
            + [pltpu.SemaphoreType.DMA((6, row_count // CHUNK))] * 2,
        ),
        out_shape=(wide,) * 6 + (sds((seq_count, 2 * RIM, chan_count), jnp.float32),),
        compiler_params=params(),
        cost_estimate=cost(100 * row_count * chan_count, 12 * size),
        name="main",
    )(
        place,
        query_first, key_first, value_first, query_second, key_second, cotangent,
        short_filter, medium_filter, tail, head,
    )
    (
        output_second,
        query_first_grad,
        key_first_grad,
        value_first_grad,
        query_second_grad,
        key_second_grad,
        parts,
    ) = results

    sums = narrowed(jnp.sum(lax.all_to_all(parts, "seq", 0, 0), axis=0))
    copies = jnp.broadcast_to(sums[None], (lax.axis_size("grp"), *sums.shape))
    table = lax.all_to_all(copies, "grp", 0, 0)
    short_grad, medium_grad = pl.pallas_call(
        unpack_kernel,
        out_shape=(
            sds(short_filter.shape, jnp.float32),
            sds(medium_filter.shape, jnp.float32),
        ),
        compiler_params=params(),
        name="unpack",
    )(table)
    return (
        output_second,
        query_first_grad,
        key_first_grad,
        value_first_grad,
        query_second_grad,
        key_second_grad,
        short_grad,
        medium_grad,
    )


def solution(mesh):
    return jax.shard_map(
        per_device,
        mesh=mesh,
        in_specs=(
            *(P("seq", "grp"),) * 6,
            P(None, None),
            P(None, None),
        ),
        out_specs=(*(P("seq", "grp"),) * 6, P(None, None), P(None, None)),
        check_vma=False,
    )
```

```python
import functools
import math

import jax
import jax.numpy as jnp
from jax import lax
from jax.experimental import pallas as pl
from jax.experimental.pallas import tpu as pltpu
from jax.sharding import PartitionSpec as P

GROUP = 16
SE_TAPS = 7
MR_TAPS = 128
BLOCK = 128
LANES = 128
RIM = 8
CHUNK = 256
HALO = 16
VMEM_LIMIT = 63 * 1024 * 1024


def widened(array):
    return array.astype(jnp.float32)


def narrowed(array):
    return array.astype(jnp.bfloat16)


def passed_along(value, axis, steps):
    count = lax.axis_size(axis)
    first, last = (max(0, -steps), min(count, count - steps))
    return lax.ppermute(value, axis, [(source, source + steps) for source in range(first, last)])


def rows_of(index, count):
    return pl.ds(pl.multiple_of(index * count, count), count)


def short_causal(prior, here, taps):
    ext = jnp.concatenate([prior, here], axis=0)
    total = taps[0:1] * here
    for shift_by in range(1, SE_TAPS):
        total += taps[shift_by : shift_by + 1] * pltpu.roll(ext, shift_by, 0)[RIM:]
    return total


def upper_lower(coefs):
    line = jnp.concatenate([coefs, jnp.zeros_like(coefs)], axis=1)
    table = jnp.broadcast_to(line, (BLOCK, 2 * BLOCK))
    return narrowed(pltpu.roll(table, 0, 1, stride=1, stride_axis=0))


def dotted(left, right, dims):
    return lax.dot_general(left, right, (dims, ((), ())), preferred_element_type=jnp.float32)


def identity(count):
    row = lax.broadcasted_iota(jnp.int32, (count, count), 0)
    lane = lax.broadcasted_iota(jnp.int32, (count, count), 1)
    return narrowed(widened(row == lane))


def turned(tile, unit):
    flat = narrowed(dotted(unit, tile, ((1,), (1,))))
    return flat.reshape(tile.shape[1] // GROUP, GROUP, tile.shape[0])


def rims_kernel(
    place_ref,
    key_tail, value_tail, query_tail, key_two_tail,
    cotangent_head, query_two_head, query_head, key_two_head,
    short_ref, medium_ref, tail_ref, head_ref,
):
    taps = widened(short_ref[...])
    start = 2 * BLOCK - BLOCK - HALO
    product_one = widened(key_tail[start:]) * widened(value_tail[start:])
    inner_one = short_causal(product_one[RIM:HALO], product_one[HALO:], taps)
    product_two = widened(key_two_tail[BLOCK:]) * (widened(query_tail[BLOCK:]) * inner_one)
    tail_ref[:HALO] = narrowed(product_one[BLOCK:])
    tail_ref[HALO:] = narrowed(product_two)
    grad_inner = narrowed(
        widened(cotangent_head[: BLOCK + HALO]) * widened(query_two_head[: BLOCK + HALO])
    )
    head_ref[:BLOCK] = grad_inner[:BLOCK]
    wide = widened(grad_inner)
    chan_count = wide.shape[1]
    group_count = chan_count // GROUP
    owner = lax.broadcasted_iota(jnp.int32, (group_count, chan_count), 1) // GROUP
    spread = narrowed(widened(owner == lax.broadcasted_iota(jnp.int32, owner.shape, 0)))
    coefs = dotted(widened(medium_ref[...]).T, widened(spread), ((1,), (0,)))
    row = lax.broadcasted_iota(jnp.int32, (HALO, chan_count), 0)
    grad_product = jnp.zeros((HALO, chan_count), jnp.float32)
    for shift_by in range(SE_TAPS - 1):
        moved = wide[:BLOCK]
        if shift_by:
            moved = pltpu.roll(wide, BLOCK + HALO - shift_by, 0)[:BLOCK]
        line = jnp.sum(coefs * moved, axis=0, keepdims=True)
        grad_product = jnp.where(row == shift_by, line, grad_product)
    head_ref[BLOCK:] = narrowed(
        grad_product * widened(key_two_head[...]) * widened(query_head[...])
    )


def copies_of(pairs, sems, chunk, size):
    rows = rows_of(chunk, size)
    return [
        pltpu.make_async_copy(source.at[rows], target.at[rows], sems.at[place, chunk])
        for place, (source, target) in enumerate(pairs)
    ]


def started(pairs, sems, chunk, size):
    for place, copy in enumerate(copies_of(pairs, sems, chunk, size)):
        copy.start(priority=place % 2)


def awaited(pairs, sems, chunk, size):
    for copy in copies_of(pairs, sems, chunk, size):
        copy.wait()


def each(count, body):
    def step(index, _):
        body(index)
        return 0

    lax.fori_loop(0, count, step, 0)


def shifted(scratch, half, index, shift_by):
    return scratch[half, pl.ds(index * BLOCK + shift_by, BLOCK)]


def gradient_kernel(
    place_ref,
    query_any, key_any, value_any, query_two_any, key_two_any, cotangent_any,
    short_ref, medium_ref, tail_ref, head_ref,
    query_grad_any, key_two_grad_any, grad_inner_any, product_any, parts_ref,
    query_ref, key_ref, value_ref, query_two_ref, key_two_ref, cotangent_ref,
    query_grad_ref, key_two_grad_ref, grad_inner_ref,
    inner_ref, gated_ref, first_ref, later_ref, pair_ref, product_ref, turned_ref, back_ref,
    coefs_ref, lines_ref, sums_ref, in_sems, out_sems, product_sem,
):
    row_count, chan_count = query_ref.shape
    group_count = chan_count // GROUP
    chunk_count = row_count // CHUNK
    span = row_count // BLOCK * GROUP
    halves = chan_count // LANES
    steps = CHUNK // BLOCK
    taps = widened(short_ref[...])
    sequence_total = row_count * lax.axis_size("seq")
    loads = (
        (key_any, key_ref), (value_any, value_ref), (query_any, query_ref),
        (key_two_any, key_two_ref), (cotangent_any, cotangent_ref), (query_two_any, query_two_ref),
    )
    saves = (
        (query_grad_ref, query_grad_any),
        (key_two_grad_ref, key_two_grad_any),
        (grad_inner_ref, grad_inner_any),
    )
    each(chunk_count, lambda chunk: started(loads, in_sems, chunk, CHUNK))

    unit = identity(chan_count)
    small_unit = unit[:BLOCK, :BLOCK]
    coefs_ref[...] = widened(medium_ref[...])
    product_ref[:, :GROUP, :] = turned(tail_ref[HALO:], unit)
    turned_ref[:, span:, :] = turned(head_ref[:BLOCK], unit)
    for half in range(halves):
        lanes = slice(half * LANES, (half + 1) * LANES)
        first_ref[half, :RIM] = widened(tail_ref[:HALO, lanes])[RIM:]
        later_ref[half, row_count:] = widened(head_ref[BLOCK:, lanes])[:RIM]

    def forward(chunk, slot):
        awaited(loads, in_sems, chunk, CHUNK)
        for step in range(steps):
            index = chunk * steps + step
            rows = rows_of(index, BLOCK)
            local = slice(step * BLOCK, (step + 1) * BLOCK)
            for half in range(halves):
                lanes = slice(half * LANES, (half + 1) * LANES)
                product_one = widened(key_ref[rows, lanes] * value_ref[rows, lanes])
                first_ref[half, pl.ds(pl.multiple_of(index * BLOCK + RIM, RIM), BLOCK)] = product_one
                inner_one = taps[0:1, lanes] * product_one
                for shift_by in range(1, SE_TAPS):
                    inner_one += taps[shift_by : shift_by + 1, lanes] * shifted(
                        first_ref, half, index, RIM - shift_by
                    )
                inner_one = narrowed(inner_one)
                gated = query_ref[rows, lanes] * inner_one
                inner_ref[rows, lanes] = inner_one
                gated_ref[rows, lanes] = gated
                pair_ref[slot, 0, local, lanes] = key_two_ref[rows, lanes] * gated
                pair_ref[slot, 1, local, lanes] = cotangent_ref[rows, lanes] * query_two_ref[rows, lanes]
        product_two = turned(pair_ref[slot, 0], unit)
        grad_inner_two = turned(pair_ref[slot, 1], unit)
        for step in range(steps):
            index = chunk * steps + step
            local = slice(step * BLOCK, (step + 1) * BLOCK)
            product_ref[:, rows_of(index + 1, GROUP), :] = product_two[:, :, local]
            turned_ref[:, rows_of(index, GROUP), :] = grad_inner_two[:, :, local]

    slots = pair_ref.shape[0]

    def forward_pair(turn):
        for slot in range(slots):
            forward(turn * slots + slot, slot)

    each(chunk_count // slots, forward_pair)
    product_copy = pltpu.make_async_copy(product_ref, product_any, product_sem)
    product_copy.start()

    flip_row = lax.broadcasted_iota(jnp.int32, (BLOCK, BLOCK), 0)
    flip_lane = lax.broadcasted_iota(jnp.int32, (BLOCK, BLOCK), 1)
    flip = narrowed(widened(flip_row + flip_lane == BLOCK - 1))
    medium_scale = 1.0 / math.sqrt(sequence_total * GROUP)

    batch = 4

    def medium_batch(turn):
        groups = [turn * batch + place for place in range(batch)]
        bands = [upper_lower(coefs_ref[pl.ds(group, 1)]) for group in groups]
        flipped = [
            narrowed(dotted(flip, product_ref[group, GROUP:], ((1,), (1,)))) for group in groups
        ]
        windows = [
            jnp.concatenate(
                [turned_ref[group, :span], turned_ref[group, GROUP : GROUP + span]], axis=1
            )
            for group in groups
        ]
        pairs = [
            dotted(left, window, ((1,), (0,))) for left, window in zip(flipped, windows)
        ]
        backs = [
            narrowed(dotted(window, band, ((1,), (1,)))) for window, band in zip(windows, bands)
        ]
        for group, back in zip(groups, backs):
            back_ref[group] = back
        for group, pair in zip(groups, pairs):
            pair = pltpu.roll(pair, BLOCK + 1, 1, stride=1, stride_axis=0)
            lines_ref[pl.ds(group, 1)] = (
                jnp.sum(pair[:, :BLOCK], axis=0, keepdims=True) * medium_scale
            )

    each(group_count // batch, medium_batch)
    sums_ref[...] = jnp.zeros_like(sums_ref)

    def backward(turn):
        chunk = chunk_count - 1 - turn
        for step in reversed(range(steps)):
            index = chunk * steps + step
            rows = rows_of(index, BLOCK)
            back = back_ref[:, rows_of(index, GROUP), :].reshape(chan_count, BLOCK)
            back = narrowed(dotted(small_unit, back, ((1,), (1,))))
            key_two_grad_ref[rows] = back * gated_ref[rows]
            grad_gated = back * key_two_ref[rows]
            query_grad_ref[rows] = grad_gated * inner_ref[rows]
            grad_inner = grad_gated * query_ref[rows]
            grad_inner_ref[rows] = grad_inner
            grad_inner = widened(grad_inner)
            for half in range(halves):
                lanes = slice(half * LANES, (half + 1) * LANES)
                here = grad_inner[:, lanes]
                later_ref[half, rows] = here
                product_one = first_ref[half, pl.ds(pl.multiple_of(index * BLOCK + RIM, RIM), BLOCK)]
                for shift_by in range(SE_TAPS):
                    moved = shifted(later_ref, half, index, shift_by) if shift_by else here
                    sums_ref[half, shift_by] += jnp.sum(
                        (product_one * moved).reshape(BLOCK // RIM, RIM, LANES), axis=0
                    )
        started(saves, out_sems, chunk, CHUNK)

    each(chunk_count, backward)

    short_scale = 1.0 / math.sqrt(sequence_total)
    per_half = LANES // GROUP
    for half in range(halves):
        lines = [
            jnp.sum(sums_ref[half, shift_by], axis=0, keepdims=True) * short_scale
            for shift_by in range(SE_TAPS)
        ]
        lines += [jnp.zeros_like(lines[0]), lines_ref[half * per_half : (half + 1) * per_half]]
        lines = jnp.concatenate(lines, axis=0)
        parts_ref[:, :, half * LANES : (half + 1) * LANES] = jnp.broadcast_to(
            lines[None], (parts_ref.shape[0], *lines.shape)
        )
    product_copy.wait()
    each(chunk_count, lambda chunk: awaited(saves, out_sems, chunk, CHUNK))


def medium_kernel(
    place_ref, product_any, query_two_any, cotangent_any, medium_ref, output_any, query_grad_any,
    product_ref, query_two_ref, cotangent_ref, output_ref, query_grad_ref, ahead_ref, coefs_ref,
    product_sems, in_sems, out_sems,
):
    row_count, chan_count = query_two_ref.shape
    chunk_count = row_count // CHUNK
    steps = CHUNK // BLOCK
    span = row_count // BLOCK * GROUP
    batch_count = product_sems.shape[1]
    batch = chan_count // GROUP // batch_count
    products = ((product_any, product_ref),)
    loads = ((query_two_any, query_two_ref), (cotangent_any, cotangent_ref))
    saves = ((output_ref, output_any), (query_grad_ref, query_grad_any))
    each(batch_count, lambda turn: started(products, product_sems, turn, batch))
    each(chunk_count, lambda chunk: started(loads, in_sems, chunk, CHUNK))
    unit = identity(BLOCK)
    coefs_ref[...] = widened(medium_ref[...])

    def medium_batch(turn):
        groups = [turn * batch + place for place in range(batch)]
        bands = [upper_lower(coefs_ref[pl.ds(group, 1)]) for group in groups]
        awaited(products, product_sems, turn, batch)
        aheads = []
        for group, band in zip(groups, bands):
            earlier = jnp.concatenate([product_ref[group, :span], product_ref[group, GROUP:]], axis=1)
            causal = jnp.concatenate([band[:, BLOCK:], band[:, :BLOCK]], axis=0)
            aheads.append(narrowed(dotted(earlier, causal, ((1,), (0,)))))
        for group, ahead in zip(groups, aheads):
            ahead_ref[group] = ahead

    each(batch_count, medium_batch)

    def one_chunk(chunk):
        awaited(loads, in_sems, chunk, CHUNK)
        for step in range(steps):
            index = chunk * steps + step
            rows = rows_of(index, BLOCK)
            ahead = ahead_ref[:, rows_of(index, GROUP), :].reshape(chan_count, BLOCK)
            ahead = narrowed(dotted(unit, ahead, ((1,), (1,))))
            output_ref[rows] = query_two_ref[rows] * ahead
            query_grad_ref[rows] = cotangent_ref[rows] * ahead
        started(saves, out_sems, chunk, CHUNK)

    each(chunk_count, one_chunk)
    each(chunk_count, lambda chunk: awaited(saves, out_sems, chunk, CHUNK))


def short_kernel(
    place_ref, grad_inner_any, key_any, value_any, short_ref, head_ref, key_grad_any, value_grad_any,
    grad_inner_ref, key_ref, value_ref, key_grad_ref, value_grad_ref, later_ref,
    in_sems, out_sems,
):
    row_count, chan_count = key_ref.shape
    chunk_count = row_count // CHUNK
    steps = CHUNK // BLOCK
    halves = chan_count // LANES
    taps = widened(short_ref[...])
    loads = ((grad_inner_any, grad_inner_ref), (key_any, key_ref), (value_any, value_ref))
    saves = ((key_grad_ref, key_grad_any), (value_grad_ref, value_grad_any))
    each(chunk_count, lambda turn: started(loads, in_sems, chunk_count - 1 - turn, CHUNK))
    for half in range(halves):
        lanes = slice(half * LANES, (half + 1) * LANES)
        later_ref[half, row_count:] = widened(head_ref[:, lanes])[:RIM]

    def backward(turn):
        chunk = chunk_count - 1 - turn
        awaited(loads, in_sems, chunk, CHUNK)
        for step in reversed(range(steps)):
            index = chunk * steps + step
            rows = rows_of(index, BLOCK)
            for half in range(halves):
                lanes = slice(half * LANES, (half + 1) * LANES)
                here = widened(grad_inner_ref[rows, lanes])
                later_ref[half, rows] = here
                total = taps[0:1, lanes] * here
                for shift_by in range(1, SE_TAPS):
                    total += taps[shift_by : shift_by + 1, lanes] * shifted(
                        later_ref, half, index, shift_by
                    )
                total = narrowed(total)
                key_grad_ref[rows, lanes] = total * value_ref[rows, lanes]
                value_grad_ref[rows, lanes] = total * key_ref[rows, lanes]
        started(saves, out_sems, chunk, CHUNK)

    each(chunk_count, backward)
    each(chunk_count, lambda chunk: awaited(saves, out_sems, chunk, CHUNK))


def unpack_kernel(table_ref, short_ref, medium_ref):
    chan_count = table_ref.shape[2]
    groups = LANES // GROUP
    for place in range(table_ref.shape[0]):
        piece = widened(table_ref[place])
        short_ref[:, place * chan_count : (place + 1) * chan_count] = piece[:SE_TAPS]
        for half in range(chan_count // LANES):
            first = (place * (chan_count // LANES) + half) * groups
            medium_ref[first : first + groups] = piece[RIM:, half * LANES : (half + 1) * LANES]


def params():
    return pltpu.CompilerParams(vmem_limit_bytes=VMEM_LIMIT)


def cost(flops, size):
    return pl.CostEstimate(flops=flops, bytes_accessed=size, transcendentals=0)


def per_device(
    query_first,
    key_first,
    value_first,
    query_second,
    key_second,
    cotangent,
    short_filter,
    medium_filter,
):
    row_count, chan_count = query_first.shape
    group_count = chan_count // GROUP
    place = lax.axis_index("grp").astype(jnp.int32).reshape(1)
    sds = jax.ShapeDtypeStruct
    wide = sds((row_count, chan_count), jnp.bfloat16)
    size = row_count * chan_count * 2

    last = row_count // (2 * BLOCK) - 1
    tail_spec = pl.BlockSpec((2 * BLOCK, chan_count), lambda i, at: (last, 0))
    head_spec = pl.BlockSpec((2 * BLOCK, chan_count), lambda i, at: (0, 0))
    rim_spec = pl.BlockSpec((HALO, chan_count), lambda i, at: (0, 0))
    halo_spec = pl.BlockSpec((HALO + BLOCK, chan_count), lambda i, at: (0, 0))
    short_spec = pl.BlockSpec((SE_TAPS, chan_count), lambda i, at: (0, at[0]))
    medium_spec = pl.BlockSpec((group_count, MR_TAPS), lambda i, at: (at[0], 0))
    halo = sds((HALO + BLOCK, chan_count), jnp.bfloat16)
    tail, head = pl.pallas_call(
        rims_kernel,
        grid_spec=pltpu.PrefetchScalarGridSpec(
            num_scalar_prefetch=1,
            grid=(1,),
            in_specs=[tail_spec] * 4 + [head_spec] * 2 + [rim_spec] * 2 + [short_spec, medium_spec],
            out_specs=(halo_spec, halo_spec),
        ),
        out_shape=(halo, halo),
        compiler_params=params(),
        cost_estimate=cost(2 * 6 * 2 * BLOCK * chan_count * 16, size),
        name="rims",
    )(
        place,
        key_first, value_first, query_first, key_second,
        cotangent, query_second, query_first, key_second,
        short_filter, medium_filter,
    )
    tail = passed_along(tail, "seq", 1)
    head = passed_along(head, "seq", -1)

    any_spec = pl.BlockSpec(memory_space=pl.ANY)
    seq_count = lax.axis_size("seq")
    lines = (row_count // BLOCK + 1) * GROUP
    halves = chan_count // LANES
    chunk_count = row_count // CHUNK
    batch_count = 4
    stream = pltpu.VMEM((row_count, chan_count), jnp.bfloat16)
    turned_stream = pltpu.VMEM((group_count, lines, BLOCK), jnp.bfloat16)
    mixed_stream = pltpu.VMEM((group_count, lines - GROUP, BLOCK), jnp.bfloat16)
    shifting = pltpu.VMEM((halves, row_count + RIM, LANES), jnp.float32)
    coefs = pltpu.VMEM((group_count, MR_TAPS), jnp.float32)
    query_first_grad, key_second_grad, grad_inner_one, product_two, parts = pl.pallas_call(
        gradient_kernel,
        grid_spec=pltpu.PrefetchScalarGridSpec(
            num_scalar_prefetch=1,
            grid=(1,),
            in_specs=[any_spec] * 6 + [short_spec, medium_spec, halo_spec, halo_spec],
            out_specs=(any_spec,) * 4
            + (pl.BlockSpec((seq_count, 2 * RIM, chan_count), lambda i, at: (0, 0, 0)),),
            scratch_shapes=[stream] * 11
            + [shifting] * 2
            + [pltpu.VMEM((2, 2, CHUNK, chan_count), jnp.bfloat16)]
            + [turned_stream] * 2
            + [mixed_stream]
            + [coefs, coefs]
            + [pltpu.VMEM((halves, SE_TAPS, RIM, LANES), jnp.float32)]
            + [
                pltpu.SemaphoreType.DMA((6, chunk_count)),
                pltpu.SemaphoreType.DMA((3, chunk_count)),
                pltpu.SemaphoreType.DMA,
            ],
        ),
        out_shape=(wide,) * 3
        + (
            sds((group_count, lines, BLOCK), jnp.bfloat16),
            sds((seq_count, 2 * RIM, chan_count), jnp.float32),
        ),
        compiler_params=params(),
        cost_estimate=cost(100 * row_count * chan_count, 10 * size),
        name="gradients",
    )(
        place,
        query_first, key_first, value_first, query_second, key_second, cotangent,
        short_filter, medium_filter, tail, head,
    )
    partials = lax.all_to_all(parts, "seq", 0, 0)
    output_second, query_second_grad = pl.pallas_call(
        medium_kernel,
        grid_spec=pltpu.PrefetchScalarGridSpec(
            num_scalar_prefetch=1,
            grid=(1,),
            in_specs=[any_spec] * 3 + [medium_spec],
            out_specs=(any_spec,) * 2,
            scratch_shapes=[turned_stream]
            + [stream] * 4
            + [mixed_stream, coefs]
            + [
                pltpu.SemaphoreType.DMA((1, batch_count)),
                pltpu.SemaphoreType.DMA((2, chunk_count)),
                pltpu.SemaphoreType.DMA((2, chunk_count)),
            ],
        ),
        out_shape=(wide,) * 2,
        compiler_params=params(),
        cost_estimate=cost(40 * row_count * chan_count, 5 * size),
        name="medium_outputs",
    )(place, product_two, query_second, cotangent, medium_filter)
    partials, output_second, query_second_grad = lax.optimization_barrier(
        (partials, output_second, query_second_grad)
    )
    sums = narrowed(jnp.sum(partials, axis=0))
    copies = jnp.broadcast_to(sums[None], (lax.axis_size("grp"), *sums.shape))
    table = lax.all_to_all(copies, "grp", 0, 0)
    rim_halo_spec = pl.BlockSpec((HALO, chan_count), lambda i, at: (BLOCK // HALO, 0))
    key_first_grad, value_first_grad = pl.pallas_call(
        short_kernel,
        grid_spec=pltpu.PrefetchScalarGridSpec(
            num_scalar_prefetch=1,
            grid=(1,),
            in_specs=[any_spec] * 3 + [short_spec, rim_halo_spec],
            out_specs=(any_spec,) * 2,
            scratch_shapes=[stream] * 5
            + [shifting]
            + [
                pltpu.SemaphoreType.DMA((3, chunk_count)),
                pltpu.SemaphoreType.DMA((2, chunk_count)),
            ],
        ),
        out_shape=(wide,) * 2,
        compiler_params=params(),
        cost_estimate=cost(40 * row_count * chan_count, 5 * size),
        name="short_outputs",
    )(place, grad_inner_one, key_first, value_first, short_filter, head)
    short_grad, medium_grad = pl.pallas_call(
        unpack_kernel,
        out_shape=(
            sds(short_filter.shape, jnp.float32),
            sds(medium_filter.shape, jnp.float32),
        ),
        name="unpack",
    )(table)
    return (
        output_second,
        query_first_grad,
        key_first_grad,
        value_first_grad,
        query_second_grad,
        key_second_grad,
        short_grad,
        medium_grad,
    )


def solution(mesh):
    return jax.shard_map(
        per_device,
        mesh=mesh,
        in_specs=(
            *(P("seq", "grp"),) * 6,
            P(None, None),
            P(None, None),
        ),
        out_specs=(*(P("seq", "grp"),) * 6, P(None, None), P(None, None)),
        check_vma=False,
    )
```

```python
import functools
import math

import jax
import jax.numpy as jnp
from jax import lax
from jax.experimental import pallas as pl
from jax.experimental.pallas import tpu as pltpu
from jax.sharding import PartitionSpec as P

GROUP = 16
SE_TAPS = 7
MR_TAPS = 128
BLOCK = 128
LANES = 128
RIM = 8
CHUNK = 256
HALO = 16
VMEM_LIMIT = 63 * 1024 * 1024


def widened(array):
    return array.astype(jnp.float32)


def narrowed(array):
    return array.astype(jnp.bfloat16)


def passed_along(value, axis, steps):
    count = lax.axis_size(axis)
    first, last = (max(0, -steps), min(count, count - steps))
    return lax.ppermute(value, axis, [(source, source + steps) for source in range(first, last)])


def rows_of(index, count):
    return pl.ds(pl.multiple_of(index * count, count), count)


def short_causal(prior, here, taps):
    ext = jnp.concatenate([prior, here], axis=0)
    total = taps[0:1] * here
    for shift_by in range(1, SE_TAPS):
        total += taps[shift_by : shift_by + 1] * pltpu.roll(ext, shift_by, 0)[RIM:]
    return total


def upper_lower(coefs):
    line = jnp.concatenate([coefs, jnp.zeros_like(coefs)], axis=1)
    table = jnp.broadcast_to(line, (BLOCK, 2 * BLOCK))
    return narrowed(pltpu.roll(table, 0, 1, stride=1, stride_axis=0))


def dotted(left, right, dims):
    return lax.dot_general(left, right, (dims, ((), ())), preferred_element_type=jnp.float32)


def identity(count):
    row = lax.broadcasted_iota(jnp.int32, (count, count), 0)
    lane = lax.broadcasted_iota(jnp.int32, (count, count), 1)
    return narrowed(widened(row == lane))


def turned(tile, unit):
    flat = narrowed(dotted(unit, tile, ((1,), (1,))))
    return flat.reshape(tile.shape[1] // GROUP, GROUP, tile.shape[0])


def rims_kernel(
    place_ref,
    key_tail, value_tail, query_tail, key_two_tail,
    cotangent_head, query_two_head, query_head, key_two_head,
    short_ref, medium_ref, tail_ref, head_ref,
):
    taps = widened(short_ref[...])
    start = 2 * BLOCK - BLOCK - HALO
    product_one = widened(key_tail[start:]) * widened(value_tail[start:])
    inner_one = short_causal(product_one[RIM:HALO], product_one[HALO:], taps)
    product_two = widened(key_two_tail[BLOCK:]) * (widened(query_tail[BLOCK:]) * inner_one)
    tail_ref[:HALO] = narrowed(product_one[BLOCK:])
    tail_ref[HALO:] = narrowed(product_two)
    grad_inner = narrowed(
        widened(cotangent_head[: BLOCK + HALO]) * widened(query_two_head[: BLOCK + HALO])
    )
    head_ref[:BLOCK] = grad_inner[:BLOCK]
    wide = widened(grad_inner)
    chan_count = wide.shape[1]
    group_count = chan_count // GROUP
    owner = lax.broadcasted_iota(jnp.int32, (group_count, chan_count), 1) // GROUP
    spread = narrowed(widened(owner == lax.broadcasted_iota(jnp.int32, owner.shape, 0)))
    coefs = dotted(widened(medium_ref[...]).T, widened(spread), ((1,), (0,)))
    row = lax.broadcasted_iota(jnp.int32, (HALO, chan_count), 0)
    grad_product = jnp.zeros((HALO, chan_count), jnp.float32)
    for shift_by in range(SE_TAPS - 1):
        moved = wide[:BLOCK]
        if shift_by:
            moved = pltpu.roll(wide, BLOCK + HALO - shift_by, 0)[:BLOCK]
        line = jnp.sum(coefs * moved, axis=0, keepdims=True)
        grad_product = jnp.where(row == shift_by, line, grad_product)
    head_ref[BLOCK:] = narrowed(
        grad_product * widened(key_two_head[...]) * widened(query_head[...])
    )


def window(scratch, start, count):
    return [scratch[pl.ds(start + place, RIM, stride=CHUNK // RIM)] for place in range(count)]


def main_kernel(
    place_ref,
    query_any, key_any, value_any, query_two_any, key_two_any, cotangent_any,
    short_ref, medium_ref, tail_ref, head_ref,
    output_any, query_grad_any, key_grad_any, value_grad_any, query_two_grad_any, key_two_grad_any,
    parts_ref,
    query_ref, key_ref, value_ref, query_two_ref, key_two_ref, cotangent_ref,
    output_ref, query_grad_ref, key_grad_ref, value_grad_ref, query_two_grad_ref, key_two_grad_ref,
    inner_ref, gated_ref, first_ref, later_ref, mixed_ref, pair_ref, product_ref, turned_ref, back_ref, ahead_ref,
    coefs_ref, lines_ref, sums_ref, in_sems, out_sems,
):
    row_count, chan_count = query_ref.shape
    group_count = chan_count // GROUP
    chunk_count = row_count // CHUNK
    span = row_count // BLOCK * GROUP
    halves = chan_count // LANES
    steps = CHUNK // BLOCK
    taps = widened(short_ref[...])
    sequence_total = row_count * lax.axis_size("seq")
    sources = (key_any, value_any, query_any, key_two_any, cotangent_any, query_two_any)
    buffers = (key_ref, value_ref, query_ref, key_two_ref, cotangent_ref, query_two_ref)
    results = (
        output_ref, query_grad_ref, key_grad_ref, value_grad_ref, query_two_grad_ref, key_two_grad_ref
    )
    targets = (
        output_any, query_grad_any, key_grad_any, value_grad_any, query_two_grad_any, key_two_grad_any
    )

    def copies_in(chunk):
        rows = rows_of(chunk, CHUNK)
        return [
            pltpu.make_async_copy(source.at[rows], buffer.at[rows], in_sems.at[place, chunk])
            for place, (source, buffer) in enumerate(zip(sources, buffers))
        ]

    def copies_out(chunk):
        rows = rows_of(chunk, CHUNK)
        return [
            pltpu.make_async_copy(result.at[rows], target.at[rows], out_sems.at[place, chunk])
            for place, (result, target) in enumerate(zip(results, targets))
        ]

    def start_in(chunk, _):
        for copy in copies_in(chunk):
            copy.start()
        return 0

    lax.fori_loop(0, chunk_count, start_in, 0)

    coefs_ref[...] = widened(medium_ref[...])
    unit = identity(chan_count)
    small_unit = unit[:BLOCK, :BLOCK]
    product_ref[:, :GROUP, :] = turned(tail_ref[HALO:], unit)
    turned_ref[:, span:, :] = turned(head_ref[:BLOCK], unit)
    for half in range(halves):
        lanes = slice(half * LANES, (half + 1) * LANES)
        first_ref[half, :RIM] = widened(tail_ref[:HALO, lanes])[RIM:]
        later_ref[half, row_count : row_count + RIM] = widened(head_ref[BLOCK:, lanes])[:RIM]

    registers = CHUNK // RIM

    def forward(chunk, _):
        for copy in copies_in(chunk):
            copy.wait()
        rows = rows_of(chunk, CHUNK)
        for half in range(halves):
            lanes = slice(half * LANES, (half + 1) * LANES)
            first, mixed = first_ref.at[half], mixed_ref.at[half]
            start = pl.multiple_of(chunk * CHUNK + RIM, RIM)
            first[pl.ds(start, CHUNK)] = widened(key_ref[rows, lanes] * value_ref[rows, lanes])
            rim = SE_TAPS - 1
            moved = window(first, start - rim, registers + rim)
            for place in range(registers):
                total = taps[0:1, lanes] * moved[place + rim]
                for shift_by in range(1, SE_TAPS):
                    total += taps[shift_by : shift_by + 1, lanes] * moved[place + rim - shift_by]
                mixed[pl.ds(place, RIM, stride=registers)] = total
            inner_one = narrowed(mixed[:CHUNK])
            gated = query_ref[rows, lanes] * inner_one
            inner_ref[rows, lanes] = inner_one
            gated_ref[rows, lanes] = gated
            pair_ref[0, :, lanes] = key_two_ref[rows, lanes] * gated
            pair_ref[1, :, lanes] = cotangent_ref[rows, lanes] * query_two_ref[rows, lanes]
        product_two = turned(pair_ref[0], unit)
        grad_inner_two = turned(pair_ref[1], unit)
        for step in range(steps):
            index = chunk * steps + step
            local = slice(step * BLOCK, (step + 1) * BLOCK)
            product_ref[:, rows_of(index + 1, GROUP), :] = product_two[:, :, local]
            turned_ref[:, rows_of(index, GROUP), :] = grad_inner_two[:, :, local]
        return 0

    lax.fori_loop(0, chunk_count, forward, 0)

    flip_row = lax.broadcasted_iota(jnp.int32, (BLOCK, BLOCK), 0)
    flip_lane = lax.broadcasted_iota(jnp.int32, (BLOCK, BLOCK), 1)
    flip = narrowed(widened(flip_row + flip_lane == BLOCK - 1))
    medium_scale = 1.0 / math.sqrt(sequence_total * GROUP)
    batch = 4

    def medium_batch(turn, _):
        groups = [turn * batch + place for place in range(batch)]
        bands = [upper_lower(coefs_ref[pl.ds(group, 1)]) for group in groups]
        flipped = [
            narrowed(dotted(flip, product_ref[group, GROUP:], ((1,), (1,)))) for group in groups
        ]
        windows = [
            jnp.concatenate(
                [turned_ref[group, :span], turned_ref[group, GROUP : GROUP + span]], axis=1
            )
            for group in groups
        ]
        pairs = [dotted(left, view, ((1,), (0,))) for left, view in zip(flipped, windows)]
        backs = [
            narrowed(dotted(view, band, ((1,), (1,)))) for view, band in zip(windows, bands)
        ]
        aheads = []
        for group, band in zip(groups, bands):
            earlier = jnp.concatenate([product_ref[group, :span], product_ref[group, GROUP:]], axis=1)
            causal = jnp.concatenate([band[:, BLOCK:], band[:, :BLOCK]], axis=0)
            aheads.append(narrowed(dotted(earlier, causal, ((1,), (0,)))))
        for group, back, ahead in zip(groups, backs, aheads):
            back_ref[group] = back
            ahead_ref[group] = ahead
        for group, pair in zip(groups, pairs):
            pair = pltpu.roll(pair, BLOCK + 1, 1, stride=1, stride_axis=0)
            lines_ref[pl.ds(group, 1)] = (
                jnp.sum(pair[:, :BLOCK], axis=0, keepdims=True) * medium_scale
            )
        return 0

    lax.fori_loop(0, group_count // batch, medium_batch, 0)
    sums_ref[...] = jnp.zeros_like(sums_ref)

    def backward(turn, _):
        chunk = chunk_count - 1 - turn
        for step in reversed(range(steps)):
            index = chunk * steps + step
            rows = rows_of(index, BLOCK)
            lines = rows_of(index, GROUP)
            back = back_ref[:, lines, :].reshape(chan_count, BLOCK)
            ahead = ahead_ref[:, lines, :].reshape(chan_count, BLOCK)
            back = narrowed(dotted(small_unit, back, ((1,), (1,))))
            ahead = narrowed(dotted(small_unit, ahead, ((1,), (1,))))
            output_ref[rows] = query_two_ref[rows] * ahead
            query_two_grad_ref[rows] = cotangent_ref[rows] * ahead
            key_two_grad_ref[rows] = back * gated_ref[rows]
            grad_gated = back * key_two_ref[rows]
            query_grad_ref[rows] = grad_gated * inner_ref[rows]
            grad_inner = widened(grad_gated * query_ref[rows])
            for half in range(halves):
                later_ref[half, rows] = grad_inner[:, half * LANES : (half + 1) * LANES]
        rows = rows_of(chunk, CHUNK)
        for half in range(halves):
            lanes = slice(half * LANES, (half + 1) * LANES)
            first, later, mixed = first_ref.at[half], later_ref.at[half], mixed_ref.at[half]
            start = pl.multiple_of(chunk * CHUNK, CHUNK)
            moved = window(later, start, registers + SE_TAPS - 1)
            sums = [sums_ref[half, shift_by] for shift_by in range(SE_TAPS)]
            for place in range(registers):
                here = first[pl.ds(start + RIM + place, RIM, stride=registers)]
                total = taps[0:1, lanes] * moved[place]
                sums[0] += here * moved[place]
                for shift_by in range(1, SE_TAPS):
                    total += taps[shift_by : shift_by + 1, lanes] * moved[place + shift_by]
                    sums[shift_by] += here * moved[place + shift_by]
                mixed[pl.ds(place, RIM, stride=registers)] = total
            for shift_by in range(SE_TAPS):
                sums_ref[half, shift_by] = sums[shift_by]
            total = narrowed(mixed[:CHUNK])
            key_grad_ref[rows, lanes] = total * value_ref[rows, lanes]
            value_grad_ref[rows, lanes] = total * key_ref[rows, lanes]
        for copy in copies_out(chunk):
            copy.start()
        return 0

    lax.fori_loop(0, chunk_count, backward, 0)

    short_scale = 1.0 / math.sqrt(sequence_total)
    per_half = LANES // GROUP
    for half in range(halves):
        lines = [
            jnp.sum(sums_ref[half, shift_by], axis=0, keepdims=True) * short_scale
            for shift_by in range(SE_TAPS)
        ]
        lines += [jnp.zeros_like(lines[0]), lines_ref[half * per_half : (half + 1) * per_half]]
        lines = jnp.concatenate(lines, axis=0)
        parts_ref[:, :, half * LANES : (half + 1) * LANES] = jnp.broadcast_to(
            lines[None], (parts_ref.shape[0], *lines.shape)
        )

    def wait_out(chunk, _):
        for copy in copies_out(chunk):
            copy.wait()
        return 0

    lax.fori_loop(0, chunk_count, wait_out, 0)


def unpack_kernel(table_ref, short_ref, medium_ref):
    chan_count = table_ref.shape[2]
    groups = LANES // GROUP
    for place in range(table_ref.shape[0]):
        piece = widened(table_ref[place])
        short_ref[:, place * chan_count : (place + 1) * chan_count] = piece[:SE_TAPS]
        for half in range(chan_count // LANES):
            first = (place * (chan_count // LANES) + half) * groups
            medium_ref[first : first + groups] = piece[RIM:, half * LANES : (half + 1) * LANES]


def params(limit=VMEM_LIMIT):
    return pltpu.CompilerParams(vmem_limit_bytes=limit)


def cost(flops, size):
    return pl.CostEstimate(flops=flops, bytes_accessed=size, transcendentals=0)


def per_device(
    query_first,
    key_first,
    value_first,
    query_second,
    key_second,
    cotangent,
    short_filter,
    medium_filter,
):
    row_count, chan_count = query_first.shape
    group_count = chan_count // GROUP
    place = lax.axis_index("grp").astype(jnp.int32).reshape(1)
    sds = jax.ShapeDtypeStruct
    wide = sds((row_count, chan_count), jnp.bfloat16)
    size = row_count * chan_count * 2

    last = row_count // (2 * BLOCK) - 1
    tail_spec = pl.BlockSpec((2 * BLOCK, chan_count), lambda i, at: (last, 0))
    head_spec = pl.BlockSpec((2 * BLOCK, chan_count), lambda i, at: (0, 0))
    rim_spec = pl.BlockSpec((HALO, chan_count), lambda i, at: (0, 0))
    halo_spec = pl.BlockSpec((HALO + BLOCK, chan_count), lambda i, at: (0, 0))
    short_spec = pl.BlockSpec((SE_TAPS, chan_count), lambda i, at: (0, at[0]))
    medium_spec = pl.BlockSpec((group_count, MR_TAPS), lambda i, at: (at[0], 0))
    halo = sds((HALO + BLOCK, chan_count), jnp.bfloat16)
    tail, head = pl.pallas_call(
        rims_kernel,
        grid_spec=pltpu.PrefetchScalarGridSpec(
            num_scalar_prefetch=1,
            grid=(1,),
            in_specs=[tail_spec] * 4 + [head_spec] * 2 + [rim_spec] * 2 + [short_spec, medium_spec],
            out_specs=(halo_spec, halo_spec),
        ),
        out_shape=(halo, halo),
        compiler_params=params(),
        cost_estimate=cost(2 * 6 * 2 * BLOCK * chan_count * 16, size),
        name="rims",
    )(
        place,
        key_first, value_first, query_first, key_second,
        cotangent, query_second, query_first, key_second,
        short_filter, medium_filter,
    )
    tail = passed_along(tail, "seq", 1)
    head = passed_along(head, "seq", -1)

    any_spec = pl.BlockSpec(memory_space=pl.ANY)
    seq_count = lax.axis_size("seq")
    lines = (row_count // BLOCK + 1) * GROUP
    halves = chan_count // LANES
    stream = pltpu.VMEM((row_count, chan_count), jnp.bfloat16)
    turned_stream = pltpu.VMEM((group_count, lines, BLOCK), jnp.bfloat16)
    results = pl.pallas_call(
        main_kernel,
        grid_spec=pltpu.PrefetchScalarGridSpec(
            num_scalar_prefetch=1,
            grid=(1,),
            in_specs=[any_spec] * 6 + [short_spec, medium_spec, halo_spec, halo_spec],
            out_specs=(any_spec,) * 6
            + (pl.BlockSpec((seq_count, 2 * RIM, chan_count), lambda i, at: (0, 0, 0)),),
            scratch_shapes=[stream] * 14
            + [pltpu.VMEM((halves, row_count + 2 * RIM + CHUNK // RIM, LANES), jnp.float32)] * 2
            + [pltpu.VMEM((halves, CHUNK + CHUNK // RIM, LANES), jnp.float32)]
            + [pltpu.VMEM((2, CHUNK, chan_count), jnp.bfloat16)]
            + [turned_stream] * 2
            + [pltpu.VMEM((group_count, lines - GROUP, BLOCK), jnp.bfloat16)] * 2
            + [pltpu.VMEM((group_count, MR_TAPS), jnp.float32)] * 2
            + [pltpu.VMEM((halves, SE_TAPS, RIM, LANES), jnp.float32)]
            + [pltpu.SemaphoreType.DMA((6, row_count // CHUNK))] * 2,
        ),
        out_shape=(wide,) * 6 + (sds((seq_count, 2 * RIM, chan_count), jnp.float32),),
        compiler_params=params(),
        cost_estimate=cost(100 * row_count * chan_count, 12 * size),
        name="main",
    )(
        place,
        query_first, key_first, value_first, query_second, key_second, cotangent,
        short_filter, medium_filter, tail, head,
    )
    (
        output_second,
        query_first_grad,
        key_first_grad,
        value_first_grad,
        query_second_grad,
        key_second_grad,
        parts,
    ) = results

    sums = narrowed(jnp.sum(lax.all_to_all(parts, "seq", 0, 0), axis=0))
    copies = jnp.broadcast_to(sums[None], (lax.axis_size("grp"), *sums.shape))
    table = lax.all_to_all(copies, "grp", 0, 0)
    short_grad, medium_grad = pl.pallas_call(
        unpack_kernel,
        out_shape=(
            sds(short_filter.shape, jnp.float32),
            sds(medium_filter.shape, jnp.float32),
        ),
        compiler_params=params(16 * 1024 * 1024),
        name="unpack",
    )(table)
    return (
        output_second,
        query_first_grad,
        key_first_grad,
        value_first_grad,
        query_second_grad,
        key_second_grad,
        short_grad,
        medium_grad,
    )


def solution(mesh):
    return jax.shard_map(
        per_device,
        mesh=mesh,
        in_specs=(
            *(P("seq", "grp"),) * 6,
            P(None, None),
            P(None, None),
        ),
        out_specs=(*(P("seq", "grp"),) * 6, P(None, None), P(None, None)),
        check_vma=False,
    )
```

```python
import functools
import math

import jax
import jax.numpy as jnp
from jax import lax
from jax.experimental import pallas as pl
from jax.experimental.pallas import tpu as pltpu
from jax.sharding import PartitionSpec as P

GROUP = 16
SE_TAPS = 7
MR_TAPS = 128
BLOCK = 128
LANES = 128
RIM = 8
CHUNK = 256
AHEAD = 4
HALO = 16
VMEM_LIMIT = 63 * 1024 * 1024


def widened(array):
    return array.astype(jnp.float32)


def narrowed(array):
    return array.astype(jnp.bfloat16)


def passed_along(value, axis, steps):
    count = lax.axis_size(axis)
    first, last = (max(0, -steps), min(count, count - steps))
    return lax.ppermute(value, axis, [(source, source + steps) for source in range(first, last)])


def rows_of(index, count):
    return pl.ds(pl.multiple_of(index * count, count), count)


def short_causal(prior, here, taps):
    ext = jnp.concatenate([prior, here], axis=0)
    total = taps[0:1] * here
    for shift_by in range(1, SE_TAPS):
        total += taps[shift_by : shift_by + 1] * pltpu.roll(ext, shift_by, 0)[RIM:]
    return total


def upper_lower(coefs):
    line = jnp.concatenate([coefs, jnp.zeros_like(coefs)], axis=1)
    table = jnp.broadcast_to(line, (BLOCK, 2 * BLOCK))
    return narrowed(pltpu.roll(table, 0, 1, stride=1, stride_axis=0))


def dotted(left, right, dims):
    return lax.dot_general(left, right, (dims, ((), ())), preferred_element_type=jnp.float32)


def identity(count):
    row = lax.broadcasted_iota(jnp.int32, (count, count), 0)
    lane = lax.broadcasted_iota(jnp.int32, (count, count), 1)
    return narrowed(widened(row == lane))


def turned(tile, unit):
    flat = narrowed(dotted(unit, tile, ((1,), (1,))))
    return flat.reshape(tile.shape[1] // GROUP, GROUP, tile.shape[0])


def rims_kernel(
    place_ref,
    key_tail, value_tail, query_tail, key_two_tail,
    cotangent_head, query_two_head, query_head, key_two_head,
    short_ref, medium_ref, tail_ref, head_ref,
):
    taps = widened(short_ref[...])
    start = 2 * BLOCK - BLOCK - HALO
    product_one = widened(key_tail[start:]) * widened(value_tail[start:])
    inner_one = short_causal(product_one[RIM:HALO], product_one[HALO:], taps)
    product_two = widened(key_two_tail[BLOCK:]) * (widened(query_tail[BLOCK:]) * inner_one)
    tail_ref[:HALO] = narrowed(product_one[BLOCK:])
    tail_ref[HALO:] = narrowed(product_two)
    grad_inner = narrowed(
        widened(cotangent_head[: BLOCK + HALO]) * widened(query_two_head[: BLOCK + HALO])
    )
    head_ref[:BLOCK] = grad_inner[:BLOCK]
    wide = widened(grad_inner)
    chan_count = wide.shape[1]
    group_count = chan_count // GROUP
    owner = lax.broadcasted_iota(jnp.int32, (group_count, chan_count), 1) // GROUP
    spread = narrowed(widened(owner == lax.broadcasted_iota(jnp.int32, owner.shape, 0)))
    coefs = dotted(widened(medium_ref[...]).T, widened(spread), ((1,), (0,)))
    row = lax.broadcasted_iota(jnp.int32, (HALO, chan_count), 0)
    grad_product = jnp.zeros((HALO, chan_count), jnp.float32)
    for shift_by in range(SE_TAPS - 1):
        moved = wide[:BLOCK]
        if shift_by:
            moved = pltpu.roll(wide, BLOCK + HALO - shift_by, 0)[:BLOCK]
        line = jnp.sum(coefs * moved, axis=0, keepdims=True)
        grad_product = jnp.where(row == shift_by, line, grad_product)
    head_ref[BLOCK:] = narrowed(
        grad_product * widened(key_two_head[...]) * widened(query_head[...])
    )


def main_kernel(
    place_ref,
    query_any, key_any, value_any, query_two_any, key_two_any, cotangent_any,
    short_ref, medium_ref, tail_ref, head_ref,
    output_any, query_grad_any, key_grad_any, value_grad_any, query_two_grad_any, key_two_grad_any,
    parts_ref,
    query_ref, key_ref, value_ref, query_two_ref, key_two_ref, cotangent_ref,
    output_ref, query_grad_ref, key_grad_ref, value_grad_ref, query_two_grad_ref, key_two_grad_ref,
    inner_ref, gated_ref, first_ref, later_ref, even_ref, odd_ref, product_ref, turned_ref, back_ref, ahead_ref,
    coefs_ref, lines_ref, sums_ref, in_sems, out_sems,
):
    row_count, chan_count = query_ref.shape
    group_count = chan_count // GROUP
    chunk_count = row_count // CHUNK
    span = row_count // BLOCK * GROUP
    halves = chan_count // LANES
    steps = CHUNK // BLOCK
    taps = widened(short_ref[...])
    sequence_total = row_count * lax.axis_size("seq")
    sources = (key_any, value_any, query_any, key_two_any, cotangent_any, query_two_any)
    buffers = (key_ref, value_ref, query_ref, key_two_ref, cotangent_ref, query_two_ref)
    results = (
        output_ref, query_grad_ref, key_grad_ref, value_grad_ref, query_two_grad_ref, key_two_grad_ref
    )
    targets = (
        output_any, query_grad_any, key_grad_any, value_grad_any, query_two_grad_any, key_two_grad_any
    )

    def copies_in(chunk):
        rows = rows_of(chunk, CHUNK)
        return [
            pltpu.make_async_copy(source.at[rows], buffer.at[rows], in_sems.at[place, chunk])
            for place, (source, buffer) in enumerate(zip(sources, buffers))
        ]

    def copies_out(chunk):
        rows = rows_of(chunk, CHUNK)
        return [
            pltpu.make_async_copy(result.at[rows], target.at[rows], out_sems.at[place, chunk])
            for place, (result, target) in enumerate(zip(results, targets))
        ]

    def start_in(chunk):
        for copy in copies_in(chunk):
            copy.start()

    for chunk in range(min(AHEAD, chunk_count)):
        start_in(chunk)

    coefs_ref[...] = widened(medium_ref[...])
    unit = identity(chan_count)
    small_unit = unit[:BLOCK, :BLOCK]
    product_ref[:, :GROUP, :] = turned(tail_ref[HALO:], unit)
    turned_ref[:, span:, :] = turned(head_ref[:BLOCK], unit)
    for half in range(halves):
        lanes = slice(half * LANES, (half + 1) * LANES)
        first_ref[half, :RIM] = widened(tail_ref[:HALO, lanes])[RIM:]
        later_ref[half, row_count:] = widened(head_ref[BLOCK:, lanes])[:RIM]

    def forward(chunk, pair_ref):
        for copy in copies_in(chunk):
            copy.wait()
        for step in range(steps):
            index = chunk * steps + step
            rows = rows_of(index, BLOCK)
            local = slice(step * BLOCK, (step + 1) * BLOCK)
            for half in range(halves):
                lanes = slice(half * LANES, (half + 1) * LANES)
                product_one = widened(key_ref[rows, lanes] * value_ref[rows, lanes])
                first_ref[half, pl.ds(pl.multiple_of(index * BLOCK + RIM, RIM), BLOCK)] = product_one
                inner_one = taps[0:1, lanes] * product_one
                for shift_by in range(1, SE_TAPS):
                    inner_one += (
                        taps[shift_by : shift_by + 1, lanes]
                        * first_ref[half, pl.ds(index * BLOCK + RIM - shift_by, BLOCK)]
                    )
                inner_one = narrowed(inner_one)
                gated = query_ref[rows, lanes] * inner_one
                inner_ref[rows, lanes] = inner_one
                gated_ref[rows, lanes] = gated
                pair_ref[0, local, lanes] = key_two_ref[rows, lanes] * gated
                pair_ref[1, local, lanes] = cotangent_ref[rows, lanes] * query_two_ref[rows, lanes]

    def turn(chunk, pair_ref):
        product_two = turned(pair_ref[0], unit)
        grad_inner_two = turned(pair_ref[1], unit)
        for step in range(steps):
            index = chunk * steps + step
            local = slice(step * BLOCK, (step + 1) * BLOCK)
            product_ref[:, rows_of(index + 1, GROUP), :] = product_two[:, :, local]
            turned_ref[:, rows_of(index, GROUP), :] = grad_inner_two[:, :, local]

    def forward_pair(count, _):
        chunk = 2 * count
        for place in range(2):

            @pl.when(chunk + AHEAD + place < chunk_count)
            def _():
                start_in(chunk + AHEAD + place)

        turn(chunk, even_ref)
        forward(chunk + 1, odd_ref)
        turn(chunk + 1, odd_ref)
        forward(chunk + 2, even_ref)
        return 0

    forward(0, even_ref)
    lax.fori_loop(0, chunk_count // 2 - 1, forward_pair, 0)
    turn(chunk_count - 2, even_ref)
    forward(chunk_count - 1, odd_ref)
    turn(chunk_count - 1, odd_ref)

    flip_row = lax.broadcasted_iota(jnp.int32, (BLOCK, BLOCK), 0)
    flip_lane = lax.broadcasted_iota(jnp.int32, (BLOCK, BLOCK), 1)
    flip = narrowed(widened(flip_row + flip_lane == BLOCK - 1))
    medium_scale = 1.0 / math.sqrt(sequence_total * GROUP)
    batch = 4

    def medium_batch(turn, _):
        groups = [turn * batch + place for place in range(batch)]
        bands = [upper_lower(coefs_ref[pl.ds(group, 1)]) for group in groups]
        flipped = [
            narrowed(dotted(flip, product_ref[group, GROUP:], ((1,), (1,)))) for group in groups
        ]
        windows = [
            jnp.concatenate(
                [turned_ref[group, :span], turned_ref[group, GROUP : GROUP + span]], axis=1
            )
            for group in groups
        ]
        pairs = [dotted(left, view, ((1,), (0,))) for left, view in zip(flipped, windows)]
        backs = [
            narrowed(dotted(view, band, ((1,), (1,)))) for view, band in zip(windows, bands)
        ]
        aheads = []
        for group, band in zip(groups, bands):
            earlier = jnp.concatenate([product_ref[group, :span], product_ref[group, GROUP:]], axis=1)
            causal = jnp.concatenate([band[:, BLOCK:], band[:, :BLOCK]], axis=0)
            aheads.append(narrowed(dotted(earlier, causal, ((1,), (0,)))))
        for group, back, ahead in zip(groups, backs, aheads):
            back_ref[group] = back
            ahead_ref[group] = ahead
        for group, pair in zip(groups, pairs):
            pair = pltpu.roll(pair, BLOCK + 1, 1, stride=1, stride_axis=0)
            lines_ref[pl.ds(group, 1)] = (
                jnp.sum(pair[:, :BLOCK], axis=0, keepdims=True) * medium_scale
            )
        return 0

    lax.fori_loop(0, group_count // batch, medium_batch, 0)
    sums_ref[...] = jnp.zeros_like(sums_ref)

    def unturn(chunk, pair_ref):
        for step in range(steps):
            lines = rows_of(chunk * steps + step, GROUP)
            local = slice(step * BLOCK, (step + 1) * BLOCK)
            back = back_ref[:, lines, :].reshape(chan_count, BLOCK)
            ahead = ahead_ref[:, lines, :].reshape(chan_count, BLOCK)
            pair_ref[0, local] = narrowed(dotted(small_unit, back, ((1,), (1,))))
            pair_ref[1, local] = narrowed(dotted(small_unit, ahead, ((1,), (1,))))

    def backward(chunk, pair_ref):
        for step in reversed(range(steps)):
            index = chunk * steps + step
            rows = rows_of(index, BLOCK)
            local = slice(step * BLOCK, (step + 1) * BLOCK)
            back = pair_ref[0, local]
            ahead = pair_ref[1, local]
            output_ref[rows] = query_two_ref[rows] * ahead
            query_two_grad_ref[rows] = cotangent_ref[rows] * ahead
            key_two_grad_ref[rows] = back * gated_ref[rows]
            grad_gated = back * key_two_ref[rows]
            query_grad_ref[rows] = grad_gated * inner_ref[rows]
            grad_inner = widened(grad_gated * query_ref[rows])
            for half in range(halves):
                lanes = slice(half * LANES, (half + 1) * LANES)
                here = grad_inner[:, lanes]
                later_ref[half, rows] = here
                product_one = first_ref[half, pl.ds(pl.multiple_of(index * BLOCK + RIM, RIM), BLOCK)]
                total = jnp.zeros_like(here)
                for shift_by in range(SE_TAPS):
                    moved = here
                    if shift_by:
                        moved = later_ref[half, pl.ds(index * BLOCK + shift_by, BLOCK)]
                    total += taps[shift_by : shift_by + 1, lanes] * moved
                    sums_ref[half, shift_by] += jnp.sum(
                        (product_one * moved).reshape(BLOCK // RIM, RIM, LANES), axis=0
                    )
                total = narrowed(total)
                key_grad_ref[rows, lanes] = total * value_ref[rows, lanes]
                value_grad_ref[rows, lanes] = total * key_ref[rows, lanes]
        for copy in copies_out(chunk):
            copy.start()

    def backward_pair(count, _):
        chunk = chunk_count - 1 - 2 * count
        unturn(chunk - 1, even_ref)
        backward(chunk, odd_ref)
        unturn(chunk - 2, odd_ref)
        backward(chunk - 1, even_ref)
        return 0

    unturn(chunk_count - 1, odd_ref)
    lax.fori_loop(0, chunk_count // 2 - 1, backward_pair, 0)
    unturn(0, even_ref)
    backward(1, odd_ref)
    backward(0, even_ref)

    short_scale = 1.0 / math.sqrt(sequence_total)
    per_half = LANES // GROUP
    for half in range(halves):
        lines = [
            jnp.sum(sums_ref[half, shift_by], axis=0, keepdims=True) * short_scale
            for shift_by in range(SE_TAPS)
        ]
        lines += [jnp.zeros_like(lines[0]), lines_ref[half * per_half : (half + 1) * per_half]]
        parts_ref[:, half * LANES : (half + 1) * LANES] = jnp.concatenate(lines, axis=0)

    def wait_out(chunk, _):
        for copy in copies_out(chunk):
            copy.wait()
        return 0

    lax.fori_loop(0, chunk_count, wait_out, 0)


def unpack_kernel(table_ref, short_ref, medium_ref):
    chan_count = table_ref.shape[2]
    groups = LANES // GROUP
    for place in range(table_ref.shape[0]):
        piece = widened(table_ref[place])
        short_ref[:, place * chan_count : (place + 1) * chan_count] = piece[:SE_TAPS]
        for half in range(chan_count // LANES):
            first = (place * (chan_count // LANES) + half) * groups
            medium_ref[first : first + groups] = piece[RIM:, half * LANES : (half + 1) * LANES]


def params(limit=VMEM_LIMIT):
    return pltpu.CompilerParams(vmem_limit_bytes=limit)


def cost(flops, size):
    return pl.CostEstimate(flops=flops, bytes_accessed=size, transcendentals=0)


def per_device(
    query_first,
    key_first,
    value_first,
    query_second,
    key_second,
    cotangent,
    short_filter,
    medium_filter,
):
    row_count, chan_count = query_first.shape
    group_count = chan_count // GROUP
    place = lax.axis_index("grp").astype(jnp.int32).reshape(1)
    sds = jax.ShapeDtypeStruct
    wide = sds((row_count, chan_count), jnp.bfloat16)
    size = row_count * chan_count * 2

    last = row_count // (2 * BLOCK) - 1
    tail_spec = pl.BlockSpec((2 * BLOCK, chan_count), lambda i, at: (last, 0))
    head_spec = pl.BlockSpec((2 * BLOCK, chan_count), lambda i, at: (0, 0))
    rim_spec = pl.BlockSpec((HALO, chan_count), lambda i, at: (0, 0))
    halo_spec = pl.BlockSpec((HALO + BLOCK, chan_count), lambda i, at: (0, 0))
    short_spec = pl.BlockSpec((SE_TAPS, chan_count), lambda i, at: (0, at[0]))
    medium_spec = pl.BlockSpec((group_count, MR_TAPS), lambda i, at: (at[0], 0))
    halo = sds((HALO + BLOCK, chan_count), jnp.bfloat16)
    tail, head = pl.pallas_call(
        rims_kernel,
        grid_spec=pltpu.PrefetchScalarGridSpec(
            num_scalar_prefetch=1,
            grid=(1,),
            in_specs=[tail_spec] * 4 + [head_spec] * 2 + [rim_spec] * 2 + [short_spec, medium_spec],
            out_specs=(halo_spec, halo_spec),
        ),
        out_shape=(halo, halo),
        compiler_params=params(),
        cost_estimate=cost(2 * 6 * 2 * BLOCK * chan_count * 16, size),
        name="rims",
    )(
        place,
        key_first, value_first, query_first, key_second,
        cotangent, query_second, query_first, key_second,
        short_filter, medium_filter,
    )
    tail = passed_along(tail, "seq", 1)
    head = passed_along(head, "seq", -1)

    any_spec = pl.BlockSpec(memory_space=pl.ANY)
    seq_count = lax.axis_size("seq")
    lines = (row_count // BLOCK + 1) * GROUP
    halves = chan_count // LANES
    stream = pltpu.VMEM((row_count, chan_count), jnp.bfloat16)
    turned_stream = pltpu.VMEM((group_count, lines, BLOCK), jnp.bfloat16)
    results = pl.pallas_call(
        main_kernel,
        grid_spec=pltpu.PrefetchScalarGridSpec(
            num_scalar_prefetch=1,
            grid=(1,),
            in_specs=[any_spec] * 6 + [short_spec, medium_spec, halo_spec, halo_spec],
            out_specs=(any_spec,) * 6
            + (pl.BlockSpec((2 * RIM, chan_count), lambda i, at: (0, 0)),),
            scratch_shapes=[stream] * 14
            + [pltpu.VMEM((halves, row_count + RIM, LANES), jnp.float32)] * 2
            + [pltpu.VMEM((2, CHUNK, chan_count), jnp.bfloat16)] * 2
            + [turned_stream] * 2
            + [pltpu.VMEM((group_count, lines - GROUP, BLOCK), jnp.bfloat16)] * 2
            + [pltpu.VMEM((group_count, MR_TAPS), jnp.float32)] * 2
            + [pltpu.VMEM((halves, SE_TAPS, RIM, LANES), jnp.float32)]
            + [pltpu.SemaphoreType.DMA((6, row_count // CHUNK))] * 2,
        ),
        out_shape=(wide,) * 6 + (sds((2 * RIM, chan_count), jnp.float32),),
        compiler_params=params(),
        cost_estimate=cost(100 * row_count * chan_count, 12 * size),
        name="main",
    )(
        place,
        query_first, key_first, value_first, query_second, key_second, cotangent,
        short_filter, medium_filter, tail, head,
    )
    (
        output_second,
        query_first_grad,
        key_first_grad,
        value_first_grad,
        query_second_grad,
        key_second_grad,
        parts,
    ) = results

    distance = 1
    while distance < seq_count:
        swaps = [(place, place ^ distance) for place in range(seq_count)]
        parts = parts + lax.ppermute(parts, "seq", swaps)
        distance *= 2
    sums = narrowed(parts)
    copies = jnp.broadcast_to(sums[None], (lax.axis_size("grp"), *sums.shape))
    table = lax.all_to_all(copies, "grp", 0, 0)
    short_grad, medium_grad = pl.pallas_call(
        unpack_kernel,
        out_shape=(
            sds(short_filter.shape, jnp.float32),
            sds(medium_filter.shape, jnp.float32),
        ),
        compiler_params=params(16 * 1024 * 1024),
        name="unpack",
    )(table)
    return (
        output_second,
        query_first_grad,
        key_first_grad,
        value_first_grad,
        query_second_grad,
        key_second_grad,
        short_grad,
        medium_grad,
    )


def solution(mesh):
    return jax.shard_map(
        per_device,
        mesh=mesh,
        in_specs=(
            *(P("seq", "grp"),) * 6,
            P(None, None),
            P(None, None),
        ),
        out_specs=(*(P("seq", "grp"),) * 6, P(None, None), P(None, None)),
        check_vma=False,
    )
```

```python
import functools
import math

import jax
import jax.numpy as jnp
from jax import lax
from jax.experimental import pallas as pl
from jax.experimental.pallas import tpu as pltpu
from jax.sharding import PartitionSpec as P

GROUP = 16
SE_TAPS = 7
MR_TAPS = 128
BLOCK = 128
LANES = 128
RIM = 8
CHUNK = 256
AHEAD = 4
HALO = 16
VMEM_LIMIT = 63 * 1024 * 1024


def widened(array):
    return array.astype(jnp.float32)


def narrowed(array):
    return array.astype(jnp.bfloat16)


def passed_along(value, axis, steps):
    count = lax.axis_size(axis)
    first, last = (max(0, -steps), min(count, count - steps))
    return lax.ppermute(value, axis, [(source, source + steps) for source in range(first, last)])


def rows_of(index, count):
    return pl.ds(pl.multiple_of(index * count, count), count)


def short_causal(prior, here, taps):
    ext = jnp.concatenate([prior, here], axis=0)
    total = taps[0:1] * here
    for shift_by in range(1, SE_TAPS):
        total += taps[shift_by : shift_by + 1] * pltpu.roll(ext, shift_by, 0)[RIM:]
    return total


def moved_lanes(tile, shift_by):
    return pltpu.roll(tile, shift_by, 1) if shift_by else tile


def upper_lower(coefs):
    line = jnp.concatenate([coefs, jnp.zeros_like(coefs)], axis=1)
    tile = jnp.broadcast_to(line, (RIM, 2 * BLOCK))
    tile = pltpu.roll(tile, 0, 1, stride=1, stride_axis=0)
    return narrowed(
        jnp.concatenate([moved_lanes(tile, first) for first in range(0, BLOCK, RIM)], axis=0)
    )


def diagonal_sums(pairs):
    total = sum(
        moved_lanes(pairs[first : first + RIM], (BLOCK + 1 + first) % (2 * BLOCK))
        for first in range(0, BLOCK, RIM)
    )
    total = pltpu.roll(total, 0, 1, stride=1, stride_axis=0)
    return jnp.sum(total[:, :BLOCK], axis=0, keepdims=True)


def dotted(left, right, dims):
    return lax.dot_general(left, right, (dims, ((), ())), preferred_element_type=jnp.float32)


def identity(count):
    row = lax.broadcasted_iota(jnp.int32, (count, count), 0)
    lane = lax.broadcasted_iota(jnp.int32, (count, count), 1)
    return narrowed(widened(row == lane))


def turned(tile, unit):
    flat = narrowed(dotted(unit, tile, ((1,), (1,))))
    return flat.reshape(tile.shape[1] // GROUP, GROUP, tile.shape[0])


def rims_kernel(
    place_ref,
    key_tail, value_tail, query_tail, key_two_tail,
    cotangent_head, query_two_head, query_head, key_two_head,
    short_ref, medium_ref, tail_ref, head_ref,
):
    taps = widened(short_ref[...])
    start = 2 * BLOCK - BLOCK - HALO
    product_one = widened(key_tail[start:]) * widened(value_tail[start:])
    inner_one = short_causal(product_one[RIM:HALO], product_one[HALO:], taps)
    product_two = widened(key_two_tail[BLOCK:]) * (widened(query_tail[BLOCK:]) * inner_one)
    tail_ref[:HALO] = narrowed(product_one[BLOCK:])
    tail_ref[HALO:] = narrowed(product_two)
    grad_inner = narrowed(
        widened(cotangent_head[: BLOCK + HALO]) * widened(query_two_head[: BLOCK + HALO])
    )
    head_ref[:BLOCK] = grad_inner[:BLOCK]
    wide = widened(grad_inner)
    chan_count = wide.shape[1]
    group_count = chan_count // GROUP
    owner = lax.broadcasted_iota(jnp.int32, (group_count, chan_count), 1) // GROUP
    spread = narrowed(widened(owner == lax.broadcasted_iota(jnp.int32, owner.shape, 0)))
    coefs = dotted(widened(medium_ref[...]).T, widened(spread), ((1,), (0,)))
    row = lax.broadcasted_iota(jnp.int32, (HALO, chan_count), 0)
    grad_product = jnp.zeros((HALO, chan_count), jnp.float32)
    for shift_by in range(SE_TAPS - 1):
        moved = wide[:BLOCK]
        if shift_by:
            moved = pltpu.roll(wide, BLOCK + HALO - shift_by, 0)[:BLOCK]
        line = jnp.sum(coefs * moved, axis=0, keepdims=True)
        grad_product = jnp.where(row == shift_by, line, grad_product)
    head_ref[BLOCK:] = narrowed(
        grad_product * widened(key_two_head[...]) * widened(query_head[...])
    )


def main_kernel(
    place_ref,
    query_any, key_any, value_any, query_two_any, key_two_any, cotangent_any,
    short_ref, medium_ref, tail_ref, head_ref,
    output_any, query_grad_any, key_grad_any, value_grad_any, query_two_grad_any, key_two_grad_any,
    parts_ref,
    query_ref, key_ref, value_ref, query_two_ref, key_two_ref, cotangent_ref,
    output_ref, query_grad_ref, key_grad_ref, value_grad_ref, query_two_grad_ref, key_two_grad_ref,
    inner_ref, gated_ref, first_ref, later_ref, even_ref, odd_ref, product_ref, turned_ref, back_ref, ahead_ref,
    coefs_ref, lines_ref, sums_ref, in_sems, out_sems,
):
    row_count, chan_count = query_ref.shape
    group_count = chan_count // GROUP
    chunk_count = row_count // CHUNK
    span = row_count // BLOCK * GROUP
    halves = chan_count // LANES
    steps = CHUNK // BLOCK
    taps = widened(short_ref[...])
    sequence_total = row_count * lax.axis_size("seq")
    sources = (key_any, value_any, query_any, key_two_any, cotangent_any, query_two_any)
    buffers = (key_ref, value_ref, query_ref, key_two_ref, cotangent_ref, query_two_ref)
    results = (
        output_ref, query_grad_ref, key_grad_ref, value_grad_ref, query_two_grad_ref, key_two_grad_ref
    )
    targets = (
        output_any, query_grad_any, key_grad_any, value_grad_any, query_two_grad_any, key_two_grad_any
    )

    def copies_in(chunk):
        rows = rows_of(chunk, CHUNK)
        return [
            pltpu.make_async_copy(source.at[rows], buffer.at[rows], in_sems.at[place, chunk])
            for place, (source, buffer) in enumerate(zip(sources, buffers))
        ]

    def copies_out(chunk):
        rows = rows_of(chunk, CHUNK)
        return [
            pltpu.make_async_copy(result.at[rows], target.at[rows], out_sems.at[place, chunk])
            for place, (result, target) in enumerate(zip(results, targets))
        ]

    def start_in(chunk):
        for copy in copies_in(chunk):
            copy.start()

    for chunk in range(min(AHEAD, chunk_count)):
        start_in(chunk)

    coefs_ref[...] = widened(medium_ref[...])
    unit = identity(chan_count)
    small_unit = unit[:BLOCK, :BLOCK]
    product_ref[:, :GROUP, :] = turned(tail_ref[HALO:], unit)
    turned_ref[:, span:, :] = turned(head_ref[:BLOCK], unit)
    for half in range(halves):
        lanes = slice(half * LANES, (half + 1) * LANES)
        first_ref[half, :RIM] = widened(tail_ref[:HALO, lanes])[RIM:]
        later_ref[half, row_count:] = widened(head_ref[BLOCK:, lanes])[:RIM]

    def forward(chunk, pair_ref):
        for copy in copies_in(chunk):
            copy.wait()
        for step in range(steps):
            index = chunk * steps + step
            rows = rows_of(index, BLOCK)
            local = slice(step * BLOCK, (step + 1) * BLOCK)
            for half in range(halves):
                lanes = slice(half * LANES, (half + 1) * LANES)
                product_one = widened(key_ref[rows, lanes] * value_ref[rows, lanes])
                first_ref[half, pl.ds(pl.multiple_of(index * BLOCK + RIM, RIM), BLOCK)] = product_one
                inner_one = taps[0:1, lanes] * product_one
                for shift_by in range(1, SE_TAPS):
                    inner_one += (
                        taps[shift_by : shift_by + 1, lanes]
                        * first_ref[half, pl.ds(index * BLOCK + RIM - shift_by, BLOCK)]
                    )
                inner_one = narrowed(inner_one)
                gated = query_ref[rows, lanes] * inner_one
                inner_ref[rows, lanes] = inner_one
                gated_ref[rows, lanes] = gated
                pair_ref[0, local, lanes] = key_two_ref[rows, lanes] * gated
                pair_ref[1, local, lanes] = cotangent_ref[rows, lanes] * query_two_ref[rows, lanes]

    def turn(chunk, pair_ref):
        product_two = turned(pair_ref[0], unit)
        grad_inner_two = turned(pair_ref[1], unit)
        for step in range(steps):
            index = chunk * steps + step
            local = slice(step * BLOCK, (step + 1) * BLOCK)
            product_ref[:, rows_of(index + 1, GROUP), :] = product_two[:, :, local]
            turned_ref[:, rows_of(index, GROUP), :] = grad_inner_two[:, :, local]

    def forward_pair(count, _):
        chunk = 2 * count
        for place in range(2):

            @pl.when(chunk + AHEAD + place < chunk_count)
            def _():
                start_in(chunk + AHEAD + place)

        turn(chunk, even_ref)
        forward(chunk + 1, odd_ref)
        turn(chunk + 1, odd_ref)
        forward(chunk + 2, even_ref)
        return 0

    forward(0, even_ref)
    lax.fori_loop(0, chunk_count // 2 - 1, forward_pair, 0)
    turn(chunk_count - 2, even_ref)
    forward(chunk_count - 1, odd_ref)
    turn(chunk_count - 1, odd_ref)

    flip_row = lax.broadcasted_iota(jnp.int32, (BLOCK, BLOCK), 0)
    flip_lane = lax.broadcasted_iota(jnp.int32, (BLOCK, BLOCK), 1)
    flip = narrowed(widened(flip_row + flip_lane == BLOCK - 1))
    medium_scale = 1.0 / math.sqrt(sequence_total * GROUP)
    batch = 4

    def medium_batch(turn, _):
        groups = [turn * batch + place for place in range(batch)]
        bands = [upper_lower(coefs_ref[pl.ds(group, 1)]) for group in groups]
        flipped = [
            narrowed(dotted(flip, product_ref[group, GROUP:], ((1,), (1,)))) for group in groups
        ]
        windows = [
            jnp.concatenate(
                [turned_ref[group, :span], turned_ref[group, GROUP : GROUP + span]], axis=1
            )
            for group in groups
        ]
        pairs = [dotted(left, view, ((1,), (0,))) for left, view in zip(flipped, windows)]
        backs = [
            narrowed(dotted(view, band, ((1,), (1,)))) for view, band in zip(windows, bands)
        ]
        aheads = []
        for group, band in zip(groups, bands):
            earlier = jnp.concatenate([product_ref[group, :span], product_ref[group, GROUP:]], axis=1)
            causal = jnp.concatenate([band[:, BLOCK:], band[:, :BLOCK]], axis=0)
            aheads.append(narrowed(dotted(earlier, causal, ((1,), (0,)))))
        for group, back, ahead in zip(groups, backs, aheads):
            back_ref[group] = back
            ahead_ref[group] = ahead
        for group, pair in zip(groups, pairs):
            lines_ref[pl.ds(group, 1)] = diagonal_sums(pair) * medium_scale
        return 0

    lax.fori_loop(0, group_count // batch, medium_batch, 0)
    sums_ref[...] = jnp.zeros_like(sums_ref)

    def unturn(chunk, pair_ref):
        for step in range(steps):
            lines = rows_of(chunk * steps + step, GROUP)
            local = slice(step * BLOCK, (step + 1) * BLOCK)
            back = back_ref[:, lines, :].reshape(chan_count, BLOCK)
            ahead = ahead_ref[:, lines, :].reshape(chan_count, BLOCK)
            pair_ref[0, local] = narrowed(dotted(small_unit, back, ((1,), (1,))))
            pair_ref[1, local] = narrowed(dotted(small_unit, ahead, ((1,), (1,))))

    def backward(chunk, pair_ref):
        for step in reversed(range(steps)):
            index = chunk * steps + step
            rows = rows_of(index, BLOCK)
            local = slice(step * BLOCK, (step + 1) * BLOCK)
            back = pair_ref[0, local]
            ahead = pair_ref[1, local]
            output_ref[rows] = query_two_ref[rows] * ahead
            query_two_grad_ref[rows] = cotangent_ref[rows] * ahead
            key_two_grad_ref[rows] = back * gated_ref[rows]
            grad_gated = back * key_two_ref[rows]
            query_grad_ref[rows] = grad_gated * inner_ref[rows]
            grad_inner = widened(grad_gated * query_ref[rows])
            for half in range(halves):
                lanes = slice(half * LANES, (half + 1) * LANES)
                here = grad_inner[:, lanes]
                later_ref[half, rows] = here
                product_one = first_ref[half, pl.ds(pl.multiple_of(index * BLOCK + RIM, RIM), BLOCK)]
                total = jnp.zeros_like(here)
                for shift_by in range(SE_TAPS):
                    moved = here
                    if shift_by:
                        moved = later_ref[half, pl.ds(index * BLOCK + shift_by, BLOCK)]
                    total += taps[shift_by : shift_by + 1, lanes] * moved
                    sums_ref[half, shift_by] += jnp.sum(
                        (product_one * moved).reshape(BLOCK // RIM, RIM, LANES), axis=0
                    )
                total = narrowed(total)
                key_grad_ref[rows, lanes] = total * value_ref[rows, lanes]
                value_grad_ref[rows, lanes] = total * key_ref[rows, lanes]
        for copy in copies_out(chunk):
            copy.start()

    def backward_pair(count, _):
        chunk = chunk_count - 1 - 2 * count
        unturn(chunk - 1, even_ref)
        backward(chunk, odd_ref)
        unturn(chunk - 2, odd_ref)
        backward(chunk - 1, even_ref)
        return 0

    unturn(chunk_count - 1, odd_ref)
    lax.fori_loop(0, chunk_count // 2 - 1, backward_pair, 0)
    unturn(0, even_ref)
    backward(1, odd_ref)
    backward(0, even_ref)

    short_scale = 1.0 / math.sqrt(sequence_total)
    per_half = LANES // GROUP
    for half in range(halves):
        lines = [
            jnp.sum(sums_ref[half, shift_by], axis=0, keepdims=True) * short_scale
            for shift_by in range(SE_TAPS)
        ]
        lines += [jnp.zeros_like(lines[0]), lines_ref[half * per_half : (half + 1) * per_half]]
        parts_ref[:, half * LANES : (half + 1) * LANES] = jnp.concatenate(lines, axis=0)

    def wait_out(chunk, _):
        for copy in copies_out(chunk):
            copy.wait()
        return 0

    lax.fori_loop(0, chunk_count, wait_out, 0)


def unpack_kernel(table_ref, short_ref, medium_ref):
    chan_count = table_ref.shape[2]
    groups = LANES // GROUP
    for place in range(table_ref.shape[0]):
        piece = widened(table_ref[place])
        short_ref[:, place * chan_count : (place + 1) * chan_count] = piece[:SE_TAPS]
        for half in range(chan_count // LANES):
            first = (place * (chan_count // LANES) + half) * groups
            medium_ref[first : first + groups] = piece[RIM:, half * LANES : (half + 1) * LANES]


def params(limit=VMEM_LIMIT):
    return pltpu.CompilerParams(vmem_limit_bytes=limit)


def cost(flops, size):
    return pl.CostEstimate(flops=flops, bytes_accessed=size, transcendentals=0)


def per_device(
    query_first,
    key_first,
    value_first,
    query_second,
    key_second,
    cotangent,
    short_filter,
    medium_filter,
):
    row_count, chan_count = query_first.shape
    group_count = chan_count // GROUP
    place = lax.axis_index("grp").astype(jnp.int32).reshape(1)
    sds = jax.ShapeDtypeStruct
    wide = sds((row_count, chan_count), jnp.bfloat16)
    size = row_count * chan_count * 2

    last = row_count // (2 * BLOCK) - 1
    tail_spec = pl.BlockSpec((2 * BLOCK, chan_count), lambda i, at: (last, 0))
    head_spec = pl.BlockSpec((2 * BLOCK, chan_count), lambda i, at: (0, 0))
    rim_spec = pl.BlockSpec((HALO, chan_count), lambda i, at: (0, 0))
    halo_spec = pl.BlockSpec((HALO + BLOCK, chan_count), lambda i, at: (0, 0))
    short_spec = pl.BlockSpec((SE_TAPS, chan_count), lambda i, at: (0, at[0]))
    medium_spec = pl.BlockSpec((group_count, MR_TAPS), lambda i, at: (at[0], 0))
    halo = sds((HALO + BLOCK, chan_count), jnp.bfloat16)
    tail, head = pl.pallas_call(
        rims_kernel,
        grid_spec=pltpu.PrefetchScalarGridSpec(
            num_scalar_prefetch=1,
            grid=(1,),
            in_specs=[tail_spec] * 4 + [head_spec] * 2 + [rim_spec] * 2 + [short_spec, medium_spec],
            out_specs=(halo_spec, halo_spec),
        ),
        out_shape=(halo, halo),
        compiler_params=params(),
        cost_estimate=cost(2 * 6 * 2 * BLOCK * chan_count * 16, size),
        name="rims",
    )(
        place,
        key_first, value_first, query_first, key_second,
        cotangent, query_second, query_first, key_second,
        short_filter, medium_filter,
    )
    tail = passed_along(tail, "seq", 1)
    head = passed_along(head, "seq", -1)

    any_spec = pl.BlockSpec(memory_space=pl.ANY)
    seq_count = lax.axis_size("seq")
    lines = (row_count // BLOCK + 1) * GROUP
    halves = chan_count // LANES
    stream = pltpu.VMEM((row_count, chan_count), jnp.bfloat16)
    turned_stream = pltpu.VMEM((group_count, lines, BLOCK), jnp.bfloat16)
    results = pl.pallas_call(
        main_kernel,
        grid_spec=pltpu.PrefetchScalarGridSpec(
            num_scalar_prefetch=1,
            grid=(1,),
            in_specs=[any_spec] * 6 + [short_spec, medium_spec, halo_spec, halo_spec],
            out_specs=(any_spec,) * 6
            + (pl.BlockSpec((2 * RIM, chan_count), lambda i, at: (0, 0)),),
            scratch_shapes=[stream] * 14
            + [pltpu.VMEM((halves, row_count + RIM, LANES), jnp.float32)] * 2
            + [pltpu.VMEM((2, CHUNK, chan_count), jnp.bfloat16)] * 2
            + [turned_stream] * 2
            + [pltpu.VMEM((group_count, lines - GROUP, BLOCK), jnp.bfloat16)] * 2
            + [pltpu.VMEM((group_count, MR_TAPS), jnp.float32)] * 2
            + [pltpu.VMEM((halves, SE_TAPS, RIM, LANES), jnp.float32)]
            + [pltpu.SemaphoreType.DMA((6, row_count // CHUNK))] * 2,
        ),
        out_shape=(wide,) * 6 + (sds((2 * RIM, chan_count), jnp.float32),),
        compiler_params=params(),
        cost_estimate=cost(100 * row_count * chan_count, 12 * size),
        name="main",
    )(
        place,
        query_first, key_first, value_first, query_second, key_second, cotangent,
        short_filter, medium_filter, tail, head,
    )
    (
        output_second,
        query_first_grad,
        key_first_grad,
        value_first_grad,
        query_second_grad,
        key_second_grad,
        parts,
    ) = results

    distance = 1
    while distance < seq_count:
        swaps = [(place, place ^ distance) for place in range(seq_count)]
        parts = parts + lax.ppermute(parts, "seq", swaps)
        distance *= 2
    sums = narrowed(parts)
    copies = jnp.broadcast_to(sums[None], (lax.axis_size("grp"), *sums.shape))
    table = lax.all_to_all(copies, "grp", 0, 0)
    short_grad, medium_grad = pl.pallas_call(
        unpack_kernel,
        out_shape=(
            sds(short_filter.shape, jnp.float32),
            sds(medium_filter.shape, jnp.float32),
        ),
        compiler_params=params(16 * 1024 * 1024),
        name="unpack",
    )(table)
    return (
        output_second,
        query_first_grad,
        key_first_grad,
        value_first_grad,
        query_second_grad,
        key_second_grad,
        short_grad,
        medium_grad,
    )


def solution(mesh):
    return jax.shard_map(
        per_device,
        mesh=mesh,
        in_specs=(
            *(P("seq", "grp"),) * 6,
            P(None, None),
            P(None, None),
        ),
        out_specs=(*(P("seq", "grp"),) * 6, P(None, None), P(None, None)),
        check_vma=False,
    )
```

```python
import functools
import math

import jax
import jax.numpy as jnp
from jax import lax
from jax.experimental import pallas as pl
from jax.experimental.pallas import tpu as pltpu
from jax.sharding import PartitionSpec as P

GROUP = 16
SE_TAPS = 7
MR_TAPS = 128
BLOCK = 128
LANES = 128
RIM = 8
CHUNK = 256
LOADS = ((0, 256), (256, 256), (512, 512), (1024, 1024))
SAVES = ((1536, 512), (1024, 512), (512, 512), (256, 256), (0, 256))
HALO = 16
VMEM_LIMIT = 63 * 1024 * 1024


def widened(array):
    return array.astype(jnp.float32)


def narrowed(array):
    return array.astype(jnp.bfloat16)


def passed_along(value, axis, steps):
    count = lax.axis_size(axis)
    first, last = (max(0, -steps), min(count, count - steps))
    return lax.ppermute(value, axis, [(source, source + steps) for source in range(first, last)])


def rows_of(index, count):
    return pl.ds(pl.multiple_of(index * count, count), count)


def short_causal(prior, here, taps):
    ext = jnp.concatenate([prior, here], axis=0)
    total = taps[0:1] * here
    for shift_by in range(1, SE_TAPS):
        total += taps[shift_by : shift_by + 1] * pltpu.roll(ext, shift_by, 0)[RIM:]
    return total


def moved_lanes(tile, shift_by):
    return pltpu.roll(tile, shift_by, 1) if shift_by else tile


def upper_lower(coefs):
    line = jnp.concatenate([coefs, jnp.zeros_like(coefs)], axis=1)
    tile = jnp.broadcast_to(line, (RIM, 2 * BLOCK))
    tile = pltpu.roll(tile, 0, 1, stride=1, stride_axis=0)
    return narrowed(
        jnp.concatenate([moved_lanes(tile, first) for first in range(0, BLOCK, RIM)], axis=0)
    )


def diagonal_sums(pairs):
    total = sum(
        moved_lanes(pairs[first : first + RIM], (BLOCK + 1 + first) % (2 * BLOCK))
        for first in range(0, BLOCK, RIM)
    )
    total = pltpu.roll(total, 0, 1, stride=1, stride_axis=0)
    return jnp.sum(total[:, :BLOCK], axis=0, keepdims=True)


def dotted(left, right, dims):
    return lax.dot_general(left, right, (dims, ((), ())), preferred_element_type=jnp.float32)


def identity(count):
    row = lax.broadcasted_iota(jnp.int32, (count, count), 0)
    lane = lax.broadcasted_iota(jnp.int32, (count, count), 1)
    return narrowed(widened(row == lane))


def turned(tile, unit):
    flat = narrowed(dotted(unit, tile, ((1,), (1,))))
    return flat.reshape(tile.shape[1] // GROUP, GROUP, tile.shape[0])


def rims_kernel(
    place_ref,
    key_tail, value_tail, query_tail, key_two_tail,
    cotangent_head, query_two_head, query_head, key_two_head,
    short_ref, medium_ref, tail_ref, head_ref,
):
    taps = widened(short_ref[...])
    start = 2 * BLOCK - BLOCK - HALO
    product_one = widened(key_tail[start:]) * widened(value_tail[start:])
    inner_one = short_causal(product_one[RIM:HALO], product_one[HALO:], taps)
    product_two = widened(key_two_tail[BLOCK:]) * (widened(query_tail[BLOCK:]) * inner_one)
    tail_ref[:HALO] = narrowed(product_one[BLOCK:])
    tail_ref[HALO:] = narrowed(product_two)
    grad_inner = narrowed(
        widened(cotangent_head[: BLOCK + HALO]) * widened(query_two_head[: BLOCK + HALO])
    )
    head_ref[:BLOCK] = grad_inner[:BLOCK]
    wide = widened(grad_inner)
    chan_count = wide.shape[1]
    group_count = chan_count // GROUP
    owner = lax.broadcasted_iota(jnp.int32, (group_count, chan_count), 1) // GROUP
    spread = narrowed(widened(owner == lax.broadcasted_iota(jnp.int32, owner.shape, 0)))
    coefs = dotted(widened(medium_ref[...]).T, widened(spread), ((1,), (0,)))
    row = lax.broadcasted_iota(jnp.int32, (HALO, chan_count), 0)
    grad_product = jnp.zeros((HALO, chan_count), jnp.float32)
    for shift_by in range(SE_TAPS - 1):
        moved = wide[:BLOCK]
        if shift_by:
            moved = pltpu.roll(wide, BLOCK + HALO - shift_by, 0)[:BLOCK]
        line = jnp.sum(coefs * moved, axis=0, keepdims=True)
        grad_product = jnp.where(row == shift_by, line, grad_product)
    head_ref[BLOCK:] = narrowed(
        grad_product * widened(key_two_head[...]) * widened(query_head[...])
    )


def main_kernel(
    place_ref,
    query_any, key_any, value_any, query_two_any, key_two_any, cotangent_any,
    short_ref, medium_ref, tail_ref, head_ref,
    output_any, query_grad_any, key_grad_any, value_grad_any, query_two_grad_any, key_two_grad_any,
    parts_ref,
    query_ref, key_ref, value_ref, query_two_ref, key_two_ref, cotangent_ref,
    output_ref, query_grad_ref, key_grad_ref, value_grad_ref, query_two_grad_ref, key_two_grad_ref,
    inner_ref, gated_ref, first_ref, later_ref, even_ref, odd_ref, product_ref, turned_ref, back_ref, ahead_ref,
    coefs_ref, lines_ref, sums_ref, in_sems, out_sems,
):
    row_count, chan_count = query_ref.shape
    group_count = chan_count // GROUP
    chunk_count = row_count // CHUNK
    span = row_count // BLOCK * GROUP
    halves = chan_count // LANES
    steps = CHUNK // BLOCK
    taps = widened(short_ref[...])
    sequence_total = row_count * lax.axis_size("seq")
    sources = (key_any, value_any, query_any, key_two_any, cotangent_any, query_two_any)
    buffers = (key_ref, value_ref, query_ref, key_two_ref, cotangent_ref, query_two_ref)
    results = (
        output_ref, query_grad_ref, key_grad_ref, value_grad_ref, query_two_grad_ref, key_two_grad_ref
    )
    targets = (
        output_any, query_grad_any, key_grad_any, value_grad_any, query_two_grad_any, key_two_grad_any
    )

    def copies_in(piece):
        rows = pl.ds(*LOADS[piece])
        return [
            pltpu.make_async_copy(source.at[rows], buffer.at[rows], in_sems.at[place, piece])
            for place, (source, buffer) in enumerate(zip(sources, buffers))
        ]

    def copies_out(piece):
        rows = pl.ds(*SAVES[piece])
        return [
            pltpu.make_async_copy(result.at[rows], target.at[rows], out_sems.at[place, piece])
            for place, (result, target) in enumerate(zip(results, targets))
        ]

    def at_chunk(chunk, pieces, act):
        for piece, (first, _) in enumerate(pieces):
            if isinstance(chunk, int):
                if chunk * CHUNK == first:
                    act(piece)
            else:
                pl.when(chunk * CHUNK == first)(functools.partial(act, piece))

    def load(piece):
        for copy in copies_in(piece):
            copy.start()

    def loaded(piece):
        for copy in copies_in(piece):
            copy.wait()

    def save(piece):
        for copy in copies_out(piece):
            copy.start()

    for piece in range(len(LOADS)):
        load(piece)

    coefs_ref[...] = widened(medium_ref[...])
    unit = identity(chan_count)
    small_unit = unit[:BLOCK, :BLOCK]
    product_ref[:, :GROUP, :] = turned(tail_ref[HALO:], unit)
    turned_ref[:, span:, :] = turned(head_ref[:BLOCK], unit)
    for half in range(halves):
        lanes = slice(half * LANES, (half + 1) * LANES)
        first_ref[half, :RIM] = widened(tail_ref[:HALO, lanes])[RIM:]
        later_ref[half, row_count:] = widened(head_ref[BLOCK:, lanes])[:RIM]

    def forward(chunk, pair_ref):
        at_chunk(chunk, LOADS, loaded)
        for step in range(steps):
            index = chunk * steps + step
            rows = rows_of(index, BLOCK)
            local = slice(step * BLOCK, (step + 1) * BLOCK)
            for half in range(halves):
                lanes = slice(half * LANES, (half + 1) * LANES)
                product_one = widened(key_ref[rows, lanes] * value_ref[rows, lanes])
                first_ref[half, pl.ds(pl.multiple_of(index * BLOCK + RIM, RIM), BLOCK)] = product_one
                inner_one = taps[0:1, lanes] * product_one
                for shift_by in range(1, SE_TAPS):
                    inner_one += (
                        taps[shift_by : shift_by + 1, lanes]
                        * first_ref[half, pl.ds(index * BLOCK + RIM - shift_by, BLOCK)]
                    )
                inner_one = narrowed(inner_one)
                gated = query_ref[rows, lanes] * inner_one
                inner_ref[rows, lanes] = inner_one
                gated_ref[rows, lanes] = gated
                pair_ref[0, local, lanes] = key_two_ref[rows, lanes] * gated
                pair_ref[1, local, lanes] = cotangent_ref[rows, lanes] * query_two_ref[rows, lanes]

    def turn(chunk, pair_ref):
        product_two = turned(pair_ref[0], unit)
        grad_inner_two = turned(pair_ref[1], unit)
        for step in range(steps):
            index = chunk * steps + step
            local = slice(step * BLOCK, (step + 1) * BLOCK)
            product_ref[:, rows_of(index + 1, GROUP), :] = product_two[:, :, local]
            turned_ref[:, rows_of(index, GROUP), :] = grad_inner_two[:, :, local]

    def forward_pair(count, _):
        chunk = 2 * count
        turn(chunk, even_ref)
        forward(chunk + 1, odd_ref)
        turn(chunk + 1, odd_ref)
        forward(chunk + 2, even_ref)
        return 0

    forward(0, even_ref)
    lax.fori_loop(0, chunk_count // 2 - 1, forward_pair, 0)
    turn(chunk_count - 2, even_ref)
    forward(chunk_count - 1, odd_ref)
    turn(chunk_count - 1, odd_ref)

    flip_row = lax.broadcasted_iota(jnp.int32, (BLOCK, BLOCK), 0)
    flip_lane = lax.broadcasted_iota(jnp.int32, (BLOCK, BLOCK), 1)
    flip = narrowed(widened(flip_row + flip_lane == BLOCK - 1))
    medium_scale = 1.0 / math.sqrt(sequence_total * GROUP)
    batch = 4

    def medium_batch(turn, _):
        groups = [turn * batch + place for place in range(batch)]
        bands = [upper_lower(coefs_ref[pl.ds(group, 1)]) for group in groups]
        flipped = [
            narrowed(dotted(flip, product_ref[group, GROUP:], ((1,), (1,)))) for group in groups
        ]
        windows = [
            jnp.concatenate(
                [turned_ref[group, :span], turned_ref[group, GROUP : GROUP + span]], axis=1
            )
            for group in groups
        ]
        pairs = [dotted(left, view, ((1,), (0,))) for left, view in zip(flipped, windows)]
        backs = [
            narrowed(dotted(view, band, ((1,), (1,)))) for view, band in zip(windows, bands)
        ]
        aheads = []
        for group, band in zip(groups, bands):
            earlier = jnp.concatenate([product_ref[group, :span], product_ref[group, GROUP:]], axis=1)
            causal = jnp.concatenate([band[:, BLOCK:], band[:, :BLOCK]], axis=0)
            aheads.append(narrowed(dotted(earlier, causal, ((1,), (0,)))))
        for group, back, ahead in zip(groups, backs, aheads):
            back_ref[group] = back
            ahead_ref[group] = ahead
        for group, pair in zip(groups, pairs):
            lines_ref[pl.ds(group, 1)] = diagonal_sums(pair) * medium_scale
        return 0

    lax.fori_loop(0, group_count // batch, medium_batch, 0)
    sums_ref[...] = jnp.zeros_like(sums_ref)

    def unturn(chunk, pair_ref):
        for step in range(steps):
            lines = rows_of(chunk * steps + step, GROUP)
            local = slice(step * BLOCK, (step + 1) * BLOCK)
            back = back_ref[:, lines, :].reshape(chan_count, BLOCK)
            ahead = ahead_ref[:, lines, :].reshape(chan_count, BLOCK)
            pair_ref[0, local] = narrowed(dotted(small_unit, back, ((1,), (1,))))
            pair_ref[1, local] = narrowed(dotted(small_unit, ahead, ((1,), (1,))))

    def backward(chunk, pair_ref):
        for step in reversed(range(steps)):
            index = chunk * steps + step
            rows = rows_of(index, BLOCK)
            local = slice(step * BLOCK, (step + 1) * BLOCK)
            back = pair_ref[0, local]
            ahead = pair_ref[1, local]
            output_ref[rows] = query_two_ref[rows] * ahead
            query_two_grad_ref[rows] = cotangent_ref[rows] * ahead
            key_two_grad_ref[rows] = back * gated_ref[rows]
            grad_gated = back * key_two_ref[rows]
            query_grad_ref[rows] = grad_gated * inner_ref[rows]
            grad_inner = widened(grad_gated * query_ref[rows])
            for half in range(halves):
                lanes = slice(half * LANES, (half + 1) * LANES)
                here = grad_inner[:, lanes]
                later_ref[half, rows] = here
                product_one = first_ref[half, pl.ds(pl.multiple_of(index * BLOCK + RIM, RIM), BLOCK)]
                total = jnp.zeros_like(here)
                for shift_by in range(SE_TAPS):
                    moved = here
                    if shift_by:
                        moved = later_ref[half, pl.ds(index * BLOCK + shift_by, BLOCK)]
                    total += taps[shift_by : shift_by + 1, lanes] * moved
                    sums_ref[half, shift_by] += jnp.sum(
                        (product_one * moved).reshape(BLOCK // RIM, RIM, LANES), axis=0
                    )
                total = narrowed(total)
                key_grad_ref[rows, lanes] = total * value_ref[rows, lanes]
                value_grad_ref[rows, lanes] = total * key_ref[rows, lanes]
        at_chunk(chunk, SAVES, save)

    def backward_pair(count, _):
        chunk = chunk_count - 1 - 2 * count
        unturn(chunk - 1, even_ref)
        backward(chunk, odd_ref)
        unturn(chunk - 2, odd_ref)
        backward(chunk - 1, even_ref)
        return 0

    unturn(chunk_count - 1, odd_ref)
    lax.fori_loop(0, chunk_count // 2 - 1, backward_pair, 0)
    unturn(0, even_ref)
    backward(1, odd_ref)
    backward(0, even_ref)

    short_scale = 1.0 / math.sqrt(sequence_total)
    per_half = LANES // GROUP
    for half in range(halves):
        lines = [
            jnp.sum(sums_ref[half, shift_by], axis=0, keepdims=True) * short_scale
            for shift_by in range(SE_TAPS)
        ]
        lines += [jnp.zeros_like(lines[0]), lines_ref[half * per_half : (half + 1) * per_half]]
        parts_ref[:, half * LANES : (half + 1) * LANES] = jnp.concatenate(lines, axis=0)

    for piece in range(len(SAVES)):
        for copy in copies_out(piece):
            copy.wait()


def unpack_kernel(table_ref, short_ref, medium_ref):
    chan_count = table_ref.shape[2]
    groups = LANES // GROUP
    for place in range(table_ref.shape[0]):
        piece = widened(table_ref[place])
        short_ref[:, place * chan_count : (place + 1) * chan_count] = piece[:SE_TAPS]
        for half in range(chan_count // LANES):
            first = (place * (chan_count // LANES) + half) * groups
            medium_ref[first : first + groups] = piece[RIM:, half * LANES : (half + 1) * LANES]


def params(limit=VMEM_LIMIT):
    return pltpu.CompilerParams(vmem_limit_bytes=limit)


def cost(flops, size):
    return pl.CostEstimate(flops=flops, bytes_accessed=size, transcendentals=0)


def per_device(
    query_first,
    key_first,
    value_first,
    query_second,
    key_second,
    cotangent,
    short_filter,
    medium_filter,
):
    row_count, chan_count = query_first.shape
    group_count = chan_count // GROUP
    place = lax.axis_index("grp").astype(jnp.int32).reshape(1)
    sds = jax.ShapeDtypeStruct
    wide = sds((row_count, chan_count), jnp.bfloat16)
    size = row_count * chan_count * 2

    last = row_count // (2 * BLOCK) - 1
    tail_spec = pl.BlockSpec((2 * BLOCK, chan_count), lambda i, at: (last, 0))
    head_spec = pl.BlockSpec((2 * BLOCK, chan_count), lambda i, at: (0, 0))
    rim_spec = pl.BlockSpec((HALO, chan_count), lambda i, at: (0, 0))
    halo_spec = pl.BlockSpec((HALO + BLOCK, chan_count), lambda i, at: (0, 0))
    short_spec = pl.BlockSpec((SE_TAPS, chan_count), lambda i, at: (0, at[0]))
    medium_spec = pl.BlockSpec((group_count, MR_TAPS), lambda i, at: (at[0], 0))
    halo = sds((HALO + BLOCK, chan_count), jnp.bfloat16)
    tail, head = pl.pallas_call(
        rims_kernel,
        grid_spec=pltpu.PrefetchScalarGridSpec(
            num_scalar_prefetch=1,
            grid=(1,),
            in_specs=[tail_spec] * 4 + [head_spec] * 2 + [rim_spec] * 2 + [short_spec, medium_spec],
            out_specs=(halo_spec, halo_spec),
        ),
        out_shape=(halo, halo),
        compiler_params=params(),
        cost_estimate=cost(2 * 6 * 2 * BLOCK * chan_count * 16, size),
        name="rims",
    )(
        place,
        key_first, value_first, query_first, key_second,
        cotangent, query_second, query_first, key_second,
        short_filter, medium_filter,
    )
    tail = passed_along(tail, "seq", 1)
    head = passed_along(head, "seq", -1)

    any_spec = pl.BlockSpec(memory_space=pl.ANY)
    seq_count = lax.axis_size("seq")
    lines = (row_count // BLOCK + 1) * GROUP
    halves = chan_count // LANES
    stream = pltpu.VMEM((row_count, chan_count), jnp.bfloat16)
    turned_stream = pltpu.VMEM((group_count, lines, BLOCK), jnp.bfloat16)
    results = pl.pallas_call(
        main_kernel,
        grid_spec=pltpu.PrefetchScalarGridSpec(
            num_scalar_prefetch=1,
            grid=(1,),
            in_specs=[any_spec] * 6 + [short_spec, medium_spec, halo_spec, halo_spec],
            out_specs=(any_spec,) * 6
            + (pl.BlockSpec((2 * RIM, chan_count), lambda i, at: (0, 0)),),
            scratch_shapes=[stream] * 14
            + [pltpu.VMEM((halves, row_count + RIM, LANES), jnp.float32)] * 2
            + [pltpu.VMEM((2, CHUNK, chan_count), jnp.bfloat16)] * 2
            + [turned_stream] * 2
            + [pltpu.VMEM((group_count, lines - GROUP, BLOCK), jnp.bfloat16)] * 2
            + [pltpu.VMEM((group_count, MR_TAPS), jnp.float32)] * 2
            + [pltpu.VMEM((halves, SE_TAPS, RIM, LANES), jnp.float32)]
            + [
                pltpu.SemaphoreType.DMA((6, len(LOADS))),
                pltpu.SemaphoreType.DMA((6, len(SAVES))),
            ],
        ),
        out_shape=(wide,) * 6 + (sds((2 * RIM, chan_count), jnp.float32),),
        compiler_params=params(),
        cost_estimate=cost(100 * row_count * chan_count, 12 * size),
        name="main",
    )(
        place,
        query_first, key_first, value_first, query_second, key_second, cotangent,
        short_filter, medium_filter, tail, head,
    )
    (
        output_second,
        query_first_grad,
        key_first_grad,
        value_first_grad,
        query_second_grad,
        key_second_grad,
        parts,
    ) = results

    distance = 1
    while distance < seq_count:
        swaps = [(place, place ^ distance) for place in range(seq_count)]
        parts = parts + lax.ppermute(parts, "seq", swaps)
        distance *= 2
    sums = narrowed(parts)
    copies = jnp.broadcast_to(sums[None], (lax.axis_size("grp"), *sums.shape))
    table = lax.all_to_all(copies, "grp", 0, 0)
    short_grad, medium_grad = pl.pallas_call(
        unpack_kernel,
        out_shape=(
            sds(short_filter.shape, jnp.float32),
            sds(medium_filter.shape, jnp.float32),
        ),
        compiler_params=params(16 * 1024 * 1024),
        name="unpack",
    )(table)
    return (
        output_second,
        query_first_grad,
        key_first_grad,
        value_first_grad,
        query_second_grad,
        key_second_grad,
        short_grad,
        medium_grad,
    )


def solution(mesh):
    return jax.shard_map(
        per_device,
        mesh=mesh,
        in_specs=(
            *(P("seq", "grp"),) * 6,
            P(None, None),
            P(None, None),
        ),
        out_specs=(*(P("seq", "grp"),) * 6, P(None, None), P(None, None)),
        check_vma=False,
    )
```

```python
import functools
import math

import jax
import jax.numpy as jnp
from jax import lax
from jax.experimental import pallas as pl
from jax.experimental.pallas import tpu as pltpu
from jax.sharding import PartitionSpec as P

GROUP = 16
SE_TAPS = 7
MR_TAPS = 128
BLOCK = 128
LANES = 128
RIM = 8
CHUNK = 256
LOADS = ((0, 256), (256, 256), (512, 512), (1024, 1024))
SAVES = ((1536, 512), (1024, 512), (512, 512), (256, 256), (0, 256))
HALO = 16
VMEM_LIMIT = 63 * 1024 * 1024


def widened(array):
    return array.astype(jnp.float32)


def narrowed(array):
    return array.astype(jnp.bfloat16)


def passed_along(value, axis, steps):
    count = lax.axis_size(axis)
    first, last = (max(0, -steps), min(count, count - steps))
    return lax.ppermute(value, axis, [(source, source + steps) for source in range(first, last)])


def rows_of(index, count):
    return pl.ds(pl.multiple_of(index * count, count), count)


def short_causal(prior, here, taps):
    ext = jnp.concatenate([prior, here], axis=0)
    total = taps[0:1] * here
    for shift_by in range(1, SE_TAPS):
        total += taps[shift_by : shift_by + 1] * pltpu.roll(ext, shift_by, 0)[RIM:]
    return total


def moved_lanes(tile, shift_by):
    return pltpu.roll(tile, shift_by, 1) if shift_by else tile


def upper_lower(coefs):
    line = jnp.concatenate([coefs, jnp.zeros_like(coefs)], axis=1)
    tile = jnp.broadcast_to(line, (RIM, 2 * BLOCK))
    tile = pltpu.roll(tile, 0, 1, stride=1, stride_axis=0)
    return narrowed(
        jnp.concatenate([moved_lanes(tile, first) for first in range(0, BLOCK, RIM)], axis=0)
    )


def diagonal_sums(pairs):
    total = sum(
        moved_lanes(pairs[first : first + RIM], (BLOCK + 1 + first) % (2 * BLOCK))
        for first in range(0, BLOCK, RIM)
    )
    total = pltpu.roll(total, 0, 1, stride=1, stride_axis=0)
    return jnp.sum(total[:, :BLOCK], axis=0, keepdims=True)


def dotted(left, right, dims):
    return lax.dot_general(left, right, (dims, ((), ())), preferred_element_type=jnp.float32)


def turned(tile):
    return tile.T.reshape(tile.shape[1] // GROUP, GROUP, tile.shape[0])


def rims_kernel(
    place_ref,
    key_tail, value_tail, query_tail, key_two_tail,
    cotangent_head, query_two_head, query_head, key_two_head,
    short_ref, medium_ref, tail_ref, head_ref,
):
    taps = widened(short_ref[...])
    start = 2 * BLOCK - BLOCK - HALO
    product_one = widened(key_tail[start:]) * widened(value_tail[start:])
    inner_one = short_causal(product_one[RIM:HALO], product_one[HALO:], taps)
    product_two = widened(key_two_tail[BLOCK:]) * (widened(query_tail[BLOCK:]) * inner_one)
    tail_ref[:HALO] = narrowed(product_one[BLOCK:])
    tail_ref[HALO:] = narrowed(product_two)
    grad_inner = narrowed(
        widened(cotangent_head[: BLOCK + HALO]) * widened(query_two_head[: BLOCK + HALO])
    )
    head_ref[:BLOCK] = grad_inner[:BLOCK]
    wide = widened(grad_inner)
    chan_count = wide.shape[1]
    group_count = chan_count // GROUP
    owner = lax.broadcasted_iota(jnp.int32, (group_count, chan_count), 1) // GROUP
    spread = narrowed(widened(owner == lax.broadcasted_iota(jnp.int32, owner.shape, 0)))
    coefs = dotted(widened(medium_ref[...]).T, widened(spread), ((1,), (0,)))
    row = lax.broadcasted_iota(jnp.int32, (HALO, chan_count), 0)
    grad_product = jnp.zeros((HALO, chan_count), jnp.float32)
    for shift_by in range(SE_TAPS - 1):
        moved = wide[:BLOCK]
        if shift_by:
            moved = pltpu.roll(wide, BLOCK + HALO - shift_by, 0)[:BLOCK]
        line = jnp.sum(coefs * moved, axis=0, keepdims=True)
        grad_product = jnp.where(row == shift_by, line, grad_product)
    head_ref[BLOCK:] = narrowed(
        grad_product * widened(key_two_head[...]) * widened(query_head[...])
    )


def main_kernel(
    place_ref,
    query_any, key_any, value_any, query_two_any, key_two_any, cotangent_any,
    short_ref, medium_ref, tail_ref, head_ref,
    output_any, query_grad_any, key_grad_any, value_grad_any, query_two_grad_any, key_two_grad_any,
    parts_ref,
    query_ref, key_ref, value_ref, query_two_ref, key_two_ref, cotangent_ref,
    output_ref, query_grad_ref, key_grad_ref, value_grad_ref, query_two_grad_ref, key_two_grad_ref,
    inner_ref, gated_ref, first_ref, later_ref, even_ref, odd_ref, product_ref, turned_ref, back_ref, ahead_ref,
    coefs_ref, lines_ref, sums_ref, in_sems, out_sems,
):
    row_count, chan_count = query_ref.shape
    group_count = chan_count // GROUP
    chunk_count = row_count // CHUNK
    span = row_count // BLOCK * GROUP
    halves = chan_count // LANES
    steps = CHUNK // BLOCK
    taps = widened(short_ref[...])
    sequence_total = row_count * lax.axis_size("seq")
    sources = (key_any, value_any, query_any, key_two_any, cotangent_any, query_two_any)
    buffers = (key_ref, value_ref, query_ref, key_two_ref, cotangent_ref, query_two_ref)
    results = (
        output_ref, query_grad_ref, key_grad_ref, value_grad_ref, query_two_grad_ref, key_two_grad_ref
    )
    targets = (
        output_any, query_grad_any, key_grad_any, value_grad_any, query_two_grad_any, key_two_grad_any
    )

    def copies_in(piece):
        rows = pl.ds(*LOADS[piece])
        return [
            pltpu.make_async_copy(source.at[rows], buffer.at[rows], in_sems.at[place, piece])
            for place, (source, buffer) in enumerate(zip(sources, buffers))
        ]

    def copies_out(piece):
        rows = pl.ds(*SAVES[piece])
        return [
            pltpu.make_async_copy(result.at[rows], target.at[rows], out_sems.at[place, piece])
            for place, (result, target) in enumerate(zip(results, targets))
        ]

    def at_chunk(chunk, pieces, act):
        for piece, (first, _) in enumerate(pieces):
            if isinstance(chunk, int):
                if chunk * CHUNK == first:
                    act(piece)
            else:
                pl.when(chunk * CHUNK == first)(functools.partial(act, piece))

    def load(piece):
        for copy in copies_in(piece):
            copy.start()

    def loaded(piece):
        for copy in copies_in(piece):
            copy.wait()

    def save(piece):
        for copy in copies_out(piece):
            copy.start()

    for piece in range(len(LOADS)):
        load(piece)

    coefs_ref[...] = widened(medium_ref[...])
    product_ref[:, :GROUP, :] = turned(tail_ref[HALO:])
    turned_ref[:, span:, :] = turned(head_ref[:BLOCK])
    for half in range(halves):
        lanes = slice(half * LANES, (half + 1) * LANES)
        first_ref[half, :RIM] = widened(tail_ref[:HALO, lanes])[RIM:]
        later_ref[half, row_count:] = widened(head_ref[BLOCK:, lanes])[:RIM]

    def forward(chunk, pair_ref):
        at_chunk(chunk, LOADS, loaded)
        for step in range(steps):
            index = chunk * steps + step
            rows = rows_of(index, BLOCK)
            local = slice(step * BLOCK, (step + 1) * BLOCK)
            for half in range(halves):
                lanes = slice(half * LANES, (half + 1) * LANES)
                product_one = widened(key_ref[rows, lanes] * value_ref[rows, lanes])
                first_ref[half, pl.ds(pl.multiple_of(index * BLOCK + RIM, RIM), BLOCK)] = product_one
                inner_one = taps[0:1, lanes] * product_one
                for shift_by in range(1, SE_TAPS):
                    inner_one += (
                        taps[shift_by : shift_by + 1, lanes]
                        * first_ref[half, pl.ds(index * BLOCK + RIM - shift_by, BLOCK)]
                    )
                inner_one = narrowed(inner_one)
                gated = query_ref[rows, lanes] * inner_one
                inner_ref[rows, lanes] = inner_one
                gated_ref[rows, lanes] = gated
                pair_ref[0, local, lanes] = key_two_ref[rows, lanes] * gated
                pair_ref[1, local, lanes] = cotangent_ref[rows, lanes] * query_two_ref[rows, lanes]

    def turn(chunk, pair_ref):
        product_two = turned(pair_ref[0])
        grad_inner_two = turned(pair_ref[1])
        for step in range(steps):
            index = chunk * steps + step
            local = slice(step * BLOCK, (step + 1) * BLOCK)
            product_ref[:, rows_of(index + 1, GROUP), :] = product_two[:, :, local]
            turned_ref[:, rows_of(index, GROUP), :] = grad_inner_two[:, :, local]

    def forward_pair(count, _):
        chunk = 2 * count
        turn(chunk, even_ref)
        forward(chunk + 1, odd_ref)
        turn(chunk + 1, odd_ref)
        forward(chunk + 2, even_ref)
        return 0

    forward(0, even_ref)
    lax.fori_loop(0, chunk_count // 2 - 1, forward_pair, 0)
    turn(chunk_count - 2, even_ref)
    forward(chunk_count - 1, odd_ref)
    turn(chunk_count - 1, odd_ref)

    flip_row = lax.broadcasted_iota(jnp.int32, (BLOCK, BLOCK), 0)
    flip_lane = lax.broadcasted_iota(jnp.int32, (BLOCK, BLOCK), 1)
    flip = narrowed(widened(flip_row + flip_lane == BLOCK - 1))
    medium_scale = 1.0 / math.sqrt(sequence_total * GROUP)
    batch = 4

    def medium_batch(turn, _):
        groups = [turn * batch + place for place in range(batch)]
        bands = [upper_lower(coefs_ref[pl.ds(group, 1)]) for group in groups]
        flipped = [
            narrowed(dotted(flip, product_ref[group, GROUP:], ((1,), (1,)))) for group in groups
        ]
        windows = [
            jnp.concatenate(
                [turned_ref[group, :span], turned_ref[group, GROUP : GROUP + span]], axis=1
            )
            for group in groups
        ]
        pairs = [dotted(left, view, ((1,), (0,))) for left, view in zip(flipped, windows)]
        backs = [
            narrowed(dotted(view, band, ((1,), (1,)))) for view, band in zip(windows, bands)
        ]
        aheads = []
        for group, band in zip(groups, bands):
            earlier = jnp.concatenate([product_ref[group, :span], product_ref[group, GROUP:]], axis=1)
            causal = jnp.concatenate([band[:, BLOCK:], band[:, :BLOCK]], axis=0)
            aheads.append(narrowed(dotted(earlier, causal, ((1,), (0,)))))
        for group, back, ahead in zip(groups, backs, aheads):
            back_ref[group] = back
            ahead_ref[group] = ahead
        for group, pair in zip(groups, pairs):
            lines_ref[pl.ds(group, 1)] = diagonal_sums(pair) * medium_scale
        return 0

    lax.fori_loop(0, group_count // batch, medium_batch, 0)
    sums_ref[...] = jnp.zeros_like(sums_ref)

    def unturn(chunk, pair_ref):
        for step in range(steps):
            lines = rows_of(chunk * steps + step, GROUP)
            local = slice(step * BLOCK, (step + 1) * BLOCK)
            back = back_ref[:, lines, :].reshape(chan_count, BLOCK)
            ahead = ahead_ref[:, lines, :].reshape(chan_count, BLOCK)
            pair_ref[0, local] = back.T
            pair_ref[1, local] = ahead.T

    def backward(chunk, pair_ref):
        for step in reversed(range(steps)):
            index = chunk * steps + step
            rows = rows_of(index, BLOCK)
            local = slice(step * BLOCK, (step + 1) * BLOCK)
            back = pair_ref[0, local]
            ahead = pair_ref[1, local]
            output_ref[rows] = query_two_ref[rows] * ahead
            query_two_grad_ref[rows] = cotangent_ref[rows] * ahead
            key_two_grad_ref[rows] = back * gated_ref[rows]
            grad_gated = back * key_two_ref[rows]
            query_grad_ref[rows] = grad_gated * inner_ref[rows]
            grad_inner = widened(grad_gated * query_ref[rows])
            for half in range(halves):
                lanes = slice(half * LANES, (half + 1) * LANES)
                here = grad_inner[:, lanes]
                later_ref[half, rows] = here
                product_one = first_ref[half, pl.ds(pl.multiple_of(index * BLOCK + RIM, RIM), BLOCK)]
                total = jnp.zeros_like(here)
                for shift_by in range(SE_TAPS):
                    moved = here
                    if shift_by:
                        moved = later_ref[half, pl.ds(index * BLOCK + shift_by, BLOCK)]
                    total += taps[shift_by : shift_by + 1, lanes] * moved
                    sums_ref[half, shift_by] += jnp.sum(
                        (product_one * moved).reshape(BLOCK // RIM, RIM, LANES), axis=0
                    )
                total = narrowed(total)
                key_grad_ref[rows, lanes] = total * value_ref[rows, lanes]
                value_grad_ref[rows, lanes] = total * key_ref[rows, lanes]
        at_chunk(chunk, SAVES, save)

    def backward_pair(count, _):
        chunk = chunk_count - 1 - 2 * count
        unturn(chunk - 1, even_ref)
        backward(chunk, odd_ref)
        unturn(chunk - 2, odd_ref)
        backward(chunk - 1, even_ref)
        return 0

    unturn(chunk_count - 1, odd_ref)
    lax.fori_loop(0, chunk_count // 2 - 1, backward_pair, 0)
    unturn(0, even_ref)
    backward(1, odd_ref)
    backward(0, even_ref)

    short_scale = 1.0 / math.sqrt(sequence_total)
    per_half = LANES // GROUP
    for half in range(halves):
        lines = [
            jnp.sum(sums_ref[half, shift_by], axis=0, keepdims=True) * short_scale
            for shift_by in range(SE_TAPS)
        ]
        lines += [jnp.zeros_like(lines[0]), lines_ref[half * per_half : (half + 1) * per_half]]
        parts_ref[:, half * LANES : (half + 1) * LANES] = jnp.concatenate(lines, axis=0)

    for piece in range(len(SAVES)):
        for copy in copies_out(piece):
            copy.wait()


def unpack_kernel(table_ref, short_ref, medium_ref):
    chan_count = table_ref.shape[2]
    groups = LANES // GROUP
    for place in range(table_ref.shape[0]):
        piece = widened(table_ref[place])
        short_ref[:, place * chan_count : (place + 1) * chan_count] = piece[:SE_TAPS]
        for half in range(chan_count // LANES):
            first = (place * (chan_count // LANES) + half) * groups
            medium_ref[first : first + groups] = piece[RIM:, half * LANES : (half + 1) * LANES]


def params(limit=VMEM_LIMIT):
    return pltpu.CompilerParams(vmem_limit_bytes=limit)


def cost(flops, size):
    return pl.CostEstimate(flops=flops, bytes_accessed=size, transcendentals=0)


def per_device(
    query_first,
    key_first,
    value_first,
    query_second,
    key_second,
    cotangent,
    short_filter,
    medium_filter,
):
    row_count, chan_count = query_first.shape
    group_count = chan_count // GROUP
    place = lax.axis_index("grp").astype(jnp.int32).reshape(1)
    sds = jax.ShapeDtypeStruct
    wide = sds((row_count, chan_count), jnp.bfloat16)
    size = row_count * chan_count * 2

    last = row_count // (2 * BLOCK) - 1
    tail_spec = pl.BlockSpec((2 * BLOCK, chan_count), lambda i, at: (last, 0))
    head_spec = pl.BlockSpec((2 * BLOCK, chan_count), lambda i, at: (0, 0))
    rim_spec = pl.BlockSpec((HALO, chan_count), lambda i, at: (0, 0))
    halo_spec = pl.BlockSpec((HALO + BLOCK, chan_count), lambda i, at: (0, 0))
    short_spec = pl.BlockSpec((SE_TAPS, chan_count), lambda i, at: (0, at[0]))
    medium_spec = pl.BlockSpec((group_count, MR_TAPS), lambda i, at: (at[0], 0))
    halo = sds((HALO + BLOCK, chan_count), jnp.bfloat16)
    tail, head = pl.pallas_call(
        rims_kernel,
        grid_spec=pltpu.PrefetchScalarGridSpec(
            num_scalar_prefetch=1,
            grid=(1,),
            in_specs=[tail_spec] * 4 + [head_spec] * 2 + [rim_spec] * 2 + [short_spec, medium_spec],
            out_specs=(halo_spec, halo_spec),
        ),
        out_shape=(halo, halo),
        compiler_params=params(),
        cost_estimate=cost(2 * 6 * 2 * BLOCK * chan_count * 16, size),
        name="rims",
    )(
        place,
        key_first, value_first, query_first, key_second,
        cotangent, query_second, query_first, key_second,
        short_filter, medium_filter,
    )
    tail = passed_along(tail, "seq", 1)
    head = passed_along(head, "seq", -1)

    any_spec = pl.BlockSpec(memory_space=pl.ANY)
    seq_count = lax.axis_size("seq")
    lines = (row_count // BLOCK + 1) * GROUP
    halves = chan_count // LANES
    stream = pltpu.VMEM((row_count, chan_count), jnp.bfloat16)
    turned_stream = pltpu.VMEM((group_count, lines, BLOCK), jnp.bfloat16)
    results = pl.pallas_call(
        main_kernel,
        grid_spec=pltpu.PrefetchScalarGridSpec(
            num_scalar_prefetch=1,
            grid=(1,),
            in_specs=[any_spec] * 6 + [short_spec, medium_spec, halo_spec, halo_spec],
            out_specs=(any_spec,) * 6
            + (pl.BlockSpec((2 * RIM, chan_count), lambda i, at: (0, 0)),),
            scratch_shapes=[stream] * 14
            + [pltpu.VMEM((halves, row_count + RIM, LANES), jnp.float32)] * 2
            + [pltpu.VMEM((2, CHUNK, chan_count), jnp.bfloat16)] * 2
            + [turned_stream] * 2
            + [pltpu.VMEM((group_count, lines - GROUP, BLOCK), jnp.bfloat16)] * 2
            + [pltpu.VMEM((group_count, MR_TAPS), jnp.float32)] * 2
            + [pltpu.VMEM((halves, SE_TAPS, RIM, LANES), jnp.float32)]
            + [
                pltpu.SemaphoreType.DMA((6, len(LOADS))),
                pltpu.SemaphoreType.DMA((6, len(SAVES))),
            ],
        ),
        out_shape=(wide,) * 6 + (sds((2 * RIM, chan_count), jnp.float32),),
        compiler_params=params(),
        cost_estimate=cost(100 * row_count * chan_count, 12 * size),
        name="main",
    )(
        place,
        query_first, key_first, value_first, query_second, key_second, cotangent,
        short_filter, medium_filter, tail, head,
    )
    (
        output_second,
        query_first_grad,
        key_first_grad,
        value_first_grad,
        query_second_grad,
        key_second_grad,
        parts,
    ) = results

    distance = 1
    while distance < seq_count:
        swaps = [(place, place ^ distance) for place in range(seq_count)]
        parts = parts + lax.ppermute(parts, "seq", swaps)
        distance *= 2
    sums = narrowed(parts)
    copies = jnp.broadcast_to(sums[None], (lax.axis_size("grp"), *sums.shape))
    table = lax.all_to_all(copies, "grp", 0, 0)
    short_grad, medium_grad = pl.pallas_call(
        unpack_kernel,
        out_shape=(
            sds(short_filter.shape, jnp.float32),
            sds(medium_filter.shape, jnp.float32),
        ),
        compiler_params=params(16 * 1024 * 1024),
        name="unpack",
    )(table)
    return (
        output_second,
        query_first_grad,
        key_first_grad,
        value_first_grad,
        query_second_grad,
        key_second_grad,
        short_grad,
        medium_grad,
    )


def solution(mesh):
    return jax.shard_map(
        per_device,
        mesh=mesh,
        in_specs=(
            *(P("seq", "grp"),) * 6,
            P(None, None),
            P(None, None),
        ),
        out_specs=(*(P("seq", "grp"),) * 6, P(None, None), P(None, None)),
        check_vma=False,
    )
```

```python
import functools
import math

import jax
import jax.numpy as jnp
from jax import lax
from jax.experimental import pallas as pl
from jax.experimental.pallas import tpu as pltpu
from jax.sharding import PartitionSpec as P

GROUP = 16
SE_TAPS = 7
MR_TAPS = 128
BLOCK = 128
LANES = 128
RIM = 8
CHUNK = 256
LOADS = ((0, 256), (256, 256), (512, 512), (1024, 1024))
SAVES = ((1536, 512), (1024, 512), (512, 512), (256, 256), (0, 256))
HALO = 16
VMEM_LIMIT = 63 * 1024 * 1024


def widened(array):
    return array.astype(jnp.float32)


def narrowed(array):
    return array.astype(jnp.bfloat16)


def passed_along(value, axis, steps):
    count = lax.axis_size(axis)
    first, last = (max(0, -steps), min(count, count - steps))
    return lax.ppermute(value, axis, [(source, source + steps) for source in range(first, last)])


def rows_of(index, count):
    return pl.ds(pl.multiple_of(index * count, count), count)


def short_causal(prior, here, taps):
    ext = jnp.concatenate([prior, here], axis=0)
    total = taps[0:1] * here
    for shift_by in range(1, SE_TAPS):
        total += taps[shift_by : shift_by + 1] * pltpu.roll(ext, shift_by, 0)[RIM:]
    return total


def moved_lanes(tile, shift_by):
    return pltpu.roll(tile, shift_by, 1) if shift_by else tile


def upper_lower(coefs):
    line = jnp.concatenate([coefs, jnp.zeros_like(coefs)], axis=1)
    tile = jnp.broadcast_to(line, (RIM, 2 * BLOCK))
    tile = pltpu.roll(tile, 0, 1, stride=1, stride_axis=0)
    return narrowed(
        jnp.concatenate([moved_lanes(tile, first) for first in range(0, BLOCK, RIM)], axis=0)
    )


def diagonal_sums(pairs):
    width = 2 * BLOCK
    total = sum(
        moved_lanes(pairs[first : first + RIM], (width - first) % width)
        for first in range(0, BLOCK, RIM)
    )
    line = sum(moved_lanes(total[row : row + 1], (width - row) % width) for row in range(RIM))
    return line[:, :BLOCK]


def dotted(left, right, dims):
    return lax.dot_general(left, right, (dims, ((), ())), preferred_element_type=jnp.float32)


def turned(tile):
    return tile.T.reshape(tile.shape[1] // GROUP, GROUP, tile.shape[0])


def rims_kernel(
    place_ref,
    key_rim, value_rim, key_tail, value_tail, query_tail, key_two_tail,
    cotangent_head, query_two_head, cotangent_rim, query_two_rim, query_head, key_two_head,
    short_ref, medium_ref, tail_ref, head_ref,
):
    taps = widened(short_ref[...])
    product_one = jnp.concatenate(
        [
            widened(key_rim[...]) * widened(value_rim[...]),
            widened(key_tail[...]) * widened(value_tail[...]),
        ],
        axis=0,
    )
    inner_one = short_causal(product_one[RIM:HALO], product_one[HALO:], taps)
    product_two = widened(key_two_tail[...]) * (widened(query_tail[...]) * inner_one)
    tail_ref[:HALO] = narrowed(product_one[BLOCK:])
    tail_ref[HALO:] = narrowed(product_two)
    grad_inner = narrowed(
        jnp.concatenate(
            [
                widened(cotangent_head[...]) * widened(query_two_head[...]),
                widened(cotangent_rim[...]) * widened(query_two_rim[...]),
            ],
            axis=0,
        )
    )
    head_ref[:BLOCK] = grad_inner[:BLOCK]
    wide = widened(grad_inner)
    chan_count = wide.shape[1]
    group_count = chan_count // GROUP
    owner = lax.broadcasted_iota(jnp.int32, (group_count, chan_count), 1) // GROUP
    spread = narrowed(widened(owner == lax.broadcasted_iota(jnp.int32, owner.shape, 0)))
    coefs = dotted(widened(medium_ref[...]).T, widened(spread), ((1,), (0,)))
    row = lax.broadcasted_iota(jnp.int32, (HALO, chan_count), 0)
    grad_product = jnp.zeros((HALO, chan_count), jnp.float32)
    for shift_by in range(SE_TAPS - 1):
        moved = wide[:BLOCK]
        if shift_by:
            moved = pltpu.roll(wide, BLOCK + HALO - shift_by, 0)[:BLOCK]
        line = jnp.sum(coefs * moved, axis=0, keepdims=True)
        grad_product = jnp.where(row == shift_by, line, grad_product)
    head_ref[BLOCK:] = narrowed(
        grad_product * widened(key_two_head[...]) * widened(query_head[...])
    )


def main_kernel(
    place_ref,
    query_any, key_any, value_any, query_two_any, key_two_any, cotangent_any,
    short_ref, medium_ref, tail_ref, head_ref,
    output_any, query_grad_any, key_grad_any, value_grad_any, query_two_grad_any, key_two_grad_any,
    parts_ref,
    query_ref, key_ref, value_ref, query_two_ref, key_two_ref, cotangent_ref,
    output_ref, query_grad_ref, key_grad_ref, value_grad_ref, query_two_grad_ref, key_two_grad_ref,
    inner_ref, gated_ref, first_ref, later_ref, even_ref, odd_ref, product_ref, turned_ref, back_ref, ahead_ref,
    coefs_ref, lines_ref, sums_ref, in_sems, out_sems,
):
    row_count, chan_count = query_ref.shape
    group_count = chan_count // GROUP
    chunk_count = row_count // CHUNK
    span = row_count // BLOCK * GROUP
    halves = chan_count // LANES
    steps = CHUNK // BLOCK
    taps = widened(short_ref[...])
    sequence_total = row_count * lax.axis_size("seq")
    sources = (key_any, value_any, query_any, key_two_any, cotangent_any, query_two_any)
    buffers = (key_ref, value_ref, query_ref, key_two_ref, cotangent_ref, query_two_ref)
    results = (
        output_ref, query_grad_ref, key_grad_ref, value_grad_ref, query_two_grad_ref, key_two_grad_ref
    )
    targets = (
        output_any, query_grad_any, key_grad_any, value_grad_any, query_two_grad_any, key_two_grad_any
    )

    def copies_in(piece):
        rows = pl.ds(*LOADS[piece])
        return [
            pltpu.make_async_copy(source.at[rows], buffer.at[rows], in_sems.at[place, piece])
            for place, (source, buffer) in enumerate(zip(sources, buffers))
        ]

    def copies_out(piece):
        rows = pl.ds(*SAVES[piece])
        return [
            pltpu.make_async_copy(result.at[rows], target.at[rows], out_sems.at[place, piece])
            for place, (result, target) in enumerate(zip(results, targets))
        ]

    def at_chunk(chunk, pieces, act):
        for piece, (first, _) in enumerate(pieces):
            if isinstance(chunk, int):
                if chunk * CHUNK == first:
                    act(piece)
            else:
                pl.when(chunk * CHUNK == first)(functools.partial(act, piece))

    def load(piece):
        for copy in copies_in(piece):
            copy.start()

    def loaded(piece):
        for copy in copies_in(piece):
            copy.wait()

    def save(piece):
        for copy in copies_out(piece):
            copy.start()

    for piece in range(len(LOADS)):
        load(piece)

    coefs_ref[...] = widened(medium_ref[...])
    product_ref[:, :GROUP, :] = turned(tail_ref[HALO:])
    turned_ref[:, span:, :] = turned(head_ref[:BLOCK])
    for half in range(halves):
        lanes = slice(half * LANES, (half + 1) * LANES)
        first_ref[half, :RIM] = widened(tail_ref[:HALO, lanes])[RIM:]
        later_ref[half, row_count:] = widened(head_ref[BLOCK:, lanes])[:RIM]

    def forward(chunk, pair_ref):
        at_chunk(chunk, LOADS, loaded)
        for step in range(steps):
            index = chunk * steps + step
            rows = rows_of(index, BLOCK)
            local = slice(step * BLOCK, (step + 1) * BLOCK)
            for half in range(halves):
                lanes = slice(half * LANES, (half + 1) * LANES)
                product_one = widened(key_ref[rows, lanes] * value_ref[rows, lanes])
                first_ref[half, pl.ds(pl.multiple_of(index * BLOCK + RIM, RIM), BLOCK)] = product_one
                inner_one = taps[0:1, lanes] * product_one
                for shift_by in range(1, SE_TAPS):
                    inner_one += (
                        taps[shift_by : shift_by + 1, lanes]
                        * first_ref[half, pl.ds(index * BLOCK + RIM - shift_by, BLOCK)]
                    )
                inner_one = narrowed(inner_one)
                gated = query_ref[rows, lanes] * inner_one
                inner_ref[rows, lanes] = inner_one
                gated_ref[rows, lanes] = gated
                pair_ref[0, local, lanes] = key_two_ref[rows, lanes] * gated
                pair_ref[1, local, lanes] = cotangent_ref[rows, lanes] * query_two_ref[rows, lanes]

    def turn(chunk, pair_ref):
        product_two = turned(pair_ref[0])
        grad_inner_two = turned(pair_ref[1])
        for step in range(steps):
            index = chunk * steps + step
            local = slice(step * BLOCK, (step + 1) * BLOCK)
            product_ref[:, rows_of(index + 1, GROUP), :] = product_two[:, :, local]
            turned_ref[:, rows_of(index, GROUP), :] = grad_inner_two[:, :, local]

    def forward_pair(count, _):
        chunk = 2 * count
        turn(chunk, even_ref)
        forward(chunk + 1, odd_ref)
        turn(chunk + 1, odd_ref)
        forward(chunk + 2, even_ref)
        return 0

    forward(0, even_ref)
    lax.fori_loop(0, chunk_count // 2 - 1, forward_pair, 0)
    turn(chunk_count - 2, even_ref)
    forward(chunk_count - 1, odd_ref)
    turn(chunk_count - 1, odd_ref)

    medium_scale = 1.0 / math.sqrt(sequence_total * GROUP)
    batch = 4

    def medium_batch(turn, _):
        groups = [turn * batch + place for place in range(batch)]
        bands = [upper_lower(coefs_ref[pl.ds(group, 1)]) for group in groups]
        flat = [
            product_ref[group, GROUP:].T for group in groups
        ]
        windows = [
            jnp.concatenate(
                [turned_ref[group, :span], turned_ref[group, GROUP : GROUP + span]], axis=1
            )
            for group in groups
        ]
        pairs = [dotted(left, view, ((1,), (0,))) for left, view in zip(flat, windows)]
        backs = [
            narrowed(dotted(view, band, ((1,), (1,)))) for view, band in zip(windows, bands)
        ]
        aheads = []
        for group, band in zip(groups, bands):
            earlier = jnp.concatenate([product_ref[group, :span], product_ref[group, GROUP:]], axis=1)
            causal = jnp.concatenate([band[:, BLOCK:], band[:, :BLOCK]], axis=0)
            aheads.append(narrowed(dotted(earlier, causal, ((1,), (0,)))))
        for group, back, ahead in zip(groups, backs, aheads):
            back_ref[group] = back
            ahead_ref[group] = ahead
        for group, pair in zip(groups, pairs):
            lines_ref[pl.ds(group, 1)] = diagonal_sums(pair) * medium_scale
        return 0

    lax.fori_loop(0, group_count // batch, medium_batch, 0)
    sums_ref[...] = jnp.zeros_like(sums_ref)

    def unturn(chunk, pair_ref):
        for step in range(steps):
            lines = rows_of(chunk * steps + step, GROUP)
            local = slice(step * BLOCK, (step + 1) * BLOCK)
            back = back_ref[:, lines, :].reshape(chan_count, BLOCK)
            ahead = ahead_ref[:, lines, :].reshape(chan_count, BLOCK)
            pair_ref[0, local] = back.T
            pair_ref[1, local] = ahead.T

    def backward(chunk, pair_ref):
        for step in reversed(range(steps)):
            index = chunk * steps + step
            rows = rows_of(index, BLOCK)
            local = slice(step * BLOCK, (step + 1) * BLOCK)
            back = pair_ref[0, local]
            ahead = pair_ref[1, local]
            output_ref[rows] = query_two_ref[rows] * ahead
            query_two_grad_ref[rows] = cotangent_ref[rows] * ahead
            key_two_grad_ref[rows] = back * gated_ref[rows]
            grad_gated = back * key_two_ref[rows]
            query_grad_ref[rows] = grad_gated * inner_ref[rows]
            grad_inner = widened(grad_gated * query_ref[rows])
            for half in range(halves):
                lanes = slice(half * LANES, (half + 1) * LANES)
                here = grad_inner[:, lanes]
                later_ref[half, rows] = here
                product_one = first_ref[half, pl.ds(pl.multiple_of(index * BLOCK + RIM, RIM), BLOCK)]
                total = jnp.zeros_like(here)
                for shift_by in range(SE_TAPS):
                    moved = here
                    if shift_by:
                        moved = later_ref[half, pl.ds(index * BLOCK + shift_by, BLOCK)]
                    total += taps[shift_by : shift_by + 1, lanes] * moved
                    sums_ref[half, shift_by] += jnp.sum(
                        (product_one * moved).reshape(BLOCK // RIM, RIM, LANES), axis=0
                    )
                total = narrowed(total)
                key_grad_ref[rows, lanes] = total * value_ref[rows, lanes]
                value_grad_ref[rows, lanes] = total * key_ref[rows, lanes]
        at_chunk(chunk, SAVES, save)

    def backward_pair(count, _):
        chunk = chunk_count - 1 - 2 * count
        unturn(chunk - 1, even_ref)
        backward(chunk, odd_ref)
        unturn(chunk - 2, odd_ref)
        backward(chunk - 1, even_ref)
        return 0

    unturn(chunk_count - 1, odd_ref)
    lax.fori_loop(0, chunk_count // 2 - 1, backward_pair, 0)
    unturn(0, even_ref)
    backward(1, odd_ref)
    backward(0, even_ref)

    short_scale = 1.0 / math.sqrt(sequence_total)
    per_half = LANES // GROUP
    for half in range(halves):
        lines = [
            jnp.sum(sums_ref[half, shift_by], axis=0, keepdims=True) * short_scale
            for shift_by in range(SE_TAPS)
        ]
        lines += [jnp.zeros_like(lines[0]), lines_ref[half * per_half : (half + 1) * per_half]]
        parts_ref[:, half * LANES : (half + 1) * LANES] = jnp.concatenate(lines, axis=0)

    for piece in range(len(SAVES)):
        for copy in copies_out(piece):
            copy.wait()


def unpack_kernel(table_ref, short_ref, medium_ref):
    chan_count = table_ref.shape[2]
    groups = LANES // GROUP
    for place in range(table_ref.shape[0]):
        piece = widened(table_ref[place])
        short_ref[:, place * chan_count : (place + 1) * chan_count] = piece[:SE_TAPS]
        for half in range(chan_count // LANES):
            first = (place * (chan_count // LANES) + half) * groups
            medium_ref[first : first + groups] = piece[RIM:, half * LANES : (half + 1) * LANES]


def params(limit=VMEM_LIMIT):
    return pltpu.CompilerParams(vmem_limit_bytes=limit)


def cost(flops, size):
    return pl.CostEstimate(flops=flops, bytes_accessed=size, transcendentals=0)


def per_device(
    query_first,
    key_first,
    value_first,
    query_second,
    key_second,
    cotangent,
    short_filter,
    medium_filter,
):
    row_count, chan_count = query_first.shape
    group_count = chan_count // GROUP
    place = lax.axis_index("grp").astype(jnp.int32).reshape(1)
    sds = jax.ShapeDtypeStruct
    wide = sds((row_count, chan_count), jnp.bfloat16)
    size = row_count * chan_count * 2

    last = row_count // BLOCK - 1
    tail_spec = pl.BlockSpec((BLOCK, chan_count), lambda i, at: (last, 0))
    head_spec = pl.BlockSpec((BLOCK, chan_count), lambda i, at: (0, 0))
    before_spec = pl.BlockSpec((HALO, chan_count), lambda i, at: (last * (BLOCK // HALO) - 1, 0))
    after_spec = pl.BlockSpec((HALO, chan_count), lambda i, at: (BLOCK // HALO, 0))
    rim_spec = pl.BlockSpec((HALO, chan_count), lambda i, at: (0, 0))
    halo_spec = pl.BlockSpec((HALO + BLOCK, chan_count), lambda i, at: (0, 0))
    short_spec = pl.BlockSpec((SE_TAPS, chan_count), lambda i, at: (0, at[0]))
    medium_spec = pl.BlockSpec((group_count, MR_TAPS), lambda i, at: (at[0], 0))
    halo = sds((HALO + BLOCK, chan_count), jnp.bfloat16)
    tail, head = pl.pallas_call(
        rims_kernel,
        grid_spec=pltpu.PrefetchScalarGridSpec(
            num_scalar_prefetch=1,
            grid=(1,),
            in_specs=[before_spec] * 2
            + [tail_spec] * 4
            + [head_spec] * 2
            + [after_spec] * 2
            + [rim_spec] * 2
            + [short_spec, medium_spec],
            out_specs=(halo_spec, halo_spec),
        ),
        out_shape=(halo, halo),
        compiler_params=params(),
        cost_estimate=cost(2 * 6 * 2 * BLOCK * chan_count * 16, size),
        name="rims",
    )(
        place,
        key_first, value_first, key_first, value_first, query_first, key_second,
        cotangent, query_second, cotangent, query_second, query_first, key_second,
        short_filter, medium_filter,
    )
    tail = passed_along(tail, "seq", 1)
    head = passed_along(head, "seq", -1)

    any_spec = pl.BlockSpec(memory_space=pl.ANY)
    seq_count = lax.axis_size("seq")
    lines = (row_count // BLOCK + 1) * GROUP
    halves = chan_count // LANES
    stream = pltpu.VMEM((row_count, chan_count), jnp.bfloat16)
    turned_stream = pltpu.VMEM((group_count, lines, BLOCK), jnp.bfloat16)
    results = pl.pallas_call(
        main_kernel,
        grid_spec=pltpu.PrefetchScalarGridSpec(
            num_scalar_prefetch=1,
            grid=(1,),
            in_specs=[any_spec] * 6 + [short_spec, medium_spec, halo_spec, halo_spec],
            out_specs=(any_spec,) * 6
            + (pl.BlockSpec((2 * RIM, chan_count), lambda i, at: (0, 0)),),
            scratch_shapes=[stream] * 14
            + [pltpu.VMEM((halves, row_count + RIM, LANES), jnp.float32)] * 2
            + [pltpu.VMEM((2, CHUNK, chan_count), jnp.bfloat16)] * 2
            + [turned_stream] * 2
            + [pltpu.VMEM((group_count, lines - GROUP, BLOCK), jnp.bfloat16)] * 2
            + [pltpu.VMEM((group_count, MR_TAPS), jnp.float32)] * 2
            + [pltpu.VMEM((halves, SE_TAPS, RIM, LANES), jnp.float32)]
            + [
                pltpu.SemaphoreType.DMA((6, len(LOADS))),
                pltpu.SemaphoreType.DMA((6, len(SAVES))),
            ],
        ),
        out_shape=(wide,) * 6 + (sds((2 * RIM, chan_count), jnp.float32),),
        compiler_params=params(),
        cost_estimate=cost(100 * row_count * chan_count, 12 * size),
        name="main",
    )(
        place,
        query_first, key_first, value_first, query_second, key_second, cotangent,
        short_filter, medium_filter, tail, head,
    )
    (
        output_second,
        query_first_grad,
        key_first_grad,
        value_first_grad,
        query_second_grad,
        key_second_grad,
        parts,
    ) = results

    distance = 1
    while distance < seq_count:
        swaps = [(place, place ^ distance) for place in range(seq_count)]
        parts = parts + lax.ppermute(parts, "seq", swaps)
        distance *= 2
    sums = narrowed(parts)
    copies = jnp.broadcast_to(sums[None], (lax.axis_size("grp"), *sums.shape))
    table = lax.all_to_all(copies, "grp", 0, 0)
    short_grad, medium_grad = pl.pallas_call(
        unpack_kernel,
        out_shape=(
            sds(short_filter.shape, jnp.float32),
            sds(medium_filter.shape, jnp.float32),
        ),
        compiler_params=params(16 * 1024 * 1024),
        name="unpack",
    )(table)
    return (
        output_second,
        query_first_grad,
        key_first_grad,
        value_first_grad,
        query_second_grad,
        key_second_grad,
        short_grad,
        medium_grad,
    )


def solution(mesh):
    return jax.shard_map(
        per_device,
        mesh=mesh,
        in_specs=(
            *(P("seq", "grp"),) * 6,
            P(None, None),
            P(None, None),
        ),
        out_specs=(*(P("seq", "grp"),) * 6, P(None, None), P(None, None)),
        check_vma=False,
    )
```
